256 devices in a mesh: prefix: 64 (over x, z, core), head: 4 (over y).
Axes of the slice: x: 4, y: 4, z: 8, core: 2. Of those that a mesh axis runs over, the one named last changes fastest.
Arguments:
- queries: bfloat16 [16384, 64, 128], P(('prefix', 'head')), may hold values from -8 to 8
- prefix_id: int32 [16384, 1], P(('prefix', 'head')), may hold values from 0 to 63; in each aligned block of 64 rows (0 to 63, 64 to 127, ...) at most 2 rows name the same one
- suffix_len: int32 [16384], P(('prefix', 'head')), may hold values from 2 to 32
- prefix_keys: bfloat16 [64, 2048, 8, 128], P('prefix', None, 'head'), may hold values from -8 to 8
- prefix_values: bfloat16 [64, 2048, 8, 128], P('prefix', None, 'head'), may hold values from -6 to 6
- suffix_keys: bfloat16 [16384, 32, 8, 128], P(('prefix', 'head')), may hold values from -8 to 8
- suffix_values: bfloat16 [16384, 32, 8, 128], P(('prefix', 'head')), may hold values from -6 to 6
- new_keys: bfloat16 [16384, 8, 128], P(('prefix', 'head')), may hold values from -8 to 8
- new_values: bfloat16 [16384, 8, 128], P(('prefix', 'head')), may hold values from -6 to 6
Outputs:
- attended: bfloat16 [16384, 64, 128], P(('prefix', 'head'))
The draws below stay inside these ranges and needn't reach their ends.
Inputs may be any that keep to these rules, and one draw needn't show every extreme that they name: `prefix_id`: the 64 rows of one device name one prefix at most 2 times.
All inputs are finite; a program needn't handle non-finite values.
Results may differ from the reference program's by a relative error of at most 0.0036.
Values may be sent and summed in bfloat16 or wider, within the bound.
A program may use at most 64 MiB of HBM per device.

```python
import math
import jax
import jax.numpy as jnp
import numpy as np
from jax import lax

QH = 64
KVH = 8
D_HEAD = 128
PREF_LEN = 2048
SUF_LEN = 32
ROWS_DEV = 64
CAP = 2
NPREF = 64
ROWS = 16384


def draw_queries(key, part):
    key = jax.random.fold_in(key, 11)
    first_key = jax.random.fold_in(key, 0)
    shape_all = (ROWS, QH, D_HEAD)
    values_out = jnp.clip(jax.random.normal(first_key, shape_all, jnp.float32), -8.0, 8.0)
    return values_out.astype(jnp.bfloat16)


def draw_prefix_keys(key, part):
    key = jax.random.fold_in(key, 13)
    shape_all = (NPREF, PREF_LEN, KVH, D_HEAD)
    values_out = jnp.clip(jax.random.normal(key, shape_all, jnp.float32), -8.0, 8.0)
    return values_out.astype(jnp.bfloat16)


def draw_suffix_keys(key, part):
    key = jax.random.fold_in(key, 17)
    shape_all = (ROWS, SUF_LEN, KVH, D_HEAD)
    values_out = jnp.clip(2.5 * jax.random.normal(key, shape_all, jnp.float32), -8.0, 8.0)
    return values_out.astype(jnp.bfloat16)


def with_ends(values, own_key, smallest, high):
    longest = values.shape.index(max(values.shape))
    spots = []
    for shift in (0, 1):
        where = [jax.random.randint(jax.random.fold_in(own_key, axis), (), 0, length) for axis, length in enumerate(values.shape)]
        where[longest] = (where[longest] + shift) % values.shape[longest]
        spots.append(tuple(where))
    return values.at[spots[0]].set(smallest).at[spots[1]].set(high)


def block_levels(stream_key, shape, cuts, least, high):
    def one(dim, shards_of):
        steps = jax.random.uniform(jax.random.fold_in(jax.random.fold_in(stream_key, 6), dim), (shards_of,), jnp.float32, least / len(cuts), high / len(cuts))
        return jnp.repeat(jnp.exp(steps), shape[dim] // shards_of).reshape((-1,) + (1,) * (len(shape) - dim - 1))

    loudness = one(*cuts[0])
    for cut in cuts[1:]:
        loudness = loudness * one(*cut)
    return loudness


def shared_out(key, own, number, rows, number_of, top, limit, lean):
    ranking = jax.random.permutation(key, number_of)
    crowded, usual = load_shares(number_of, rows * top, limit, lean, True), load_shares(number_of, rows * top, limit, lean, False)
    places = jnp.arange(number_of)

    def named(lengths, rotation):
        used = int((lengths > 0).sum())
        fixed = max(1, used // 4)
        shifted = fixed + (places - fixed + rotation * (used - fixed)) % max(1, number_of - fixed)
        return jnp.zeros((number_of,), jnp.int32).at[ranking[jnp.where(places < fixed, places, shifted)]].set(jnp.asarray(lengths, jnp.int32))

    lengths = jnp.where(number % 4 == 0, named(crowded, number // 4), named(usual, number - number // 4 - 1))
    mixed = jax.random.permutation(jax.random.fold_in(own, 3), number_of)
    giver, taker = mixed[0:number_of // 2 * 2:2], mixed[1:number_of // 2 * 2:2]
    slack = jnp.minimum(lengths[giver] - 1, limit - lengths[taker]) // 2
    slack = jnp.where((giver == ranking[0]) | (taker == ranking[0]) | (lengths[taker] == 0), 0, jnp.maximum(slack, 0))
    shifted = jax.random.randint(jax.random.fold_in(own, 4), (number_of // 2,), 0, 1 << 20) % (slack + 1)
    lengths = lengths.at[giver].add(-shifted).at[taker].add(shifted)
    members = jnp.searchsorted(jnp.cumsum(lengths), jnp.arange(rows * top), side="right").astype(jnp.int32)
    table = members.reshape(top, rows).T
    table = table[jax.random.permutation(jax.random.fold_in(own, 1), rows)]
    rotation = jax.random.randint(jax.random.fold_in(own, 2), (rows, 1), 0, top)
    return jnp.take_along_axis(table, (jnp.arange(top)[None, :] + rotation) % top, axis=1)


def load_shares(count, total, most, lean, full):
    loads = [(1 << 20) // math.isqrt(grade ** lean) + 1 for grade in range(1, count + 1)]
    largest = most if full else min(most, max(-(-total // count), total * loads[0] // sum(loads)))
    least = 1 if total - largest >= count - 1 else 0
    counts, surplus = [largest] + [least] * (count - 1), total - largest - least * (count - 1)
    while surplus > 0:
        free = [i for i in range(1, count) if counts[i] < largest] or [i for i in range(1, count) if counts[i] < most]
        pool, remaining = sum([loads[i] for i in free]), surplus
        for i in free:
            more = min(most - counts[i], max(1, remaining * loads[i] // pool), surplus)
            counts[i] = counts[i] + more
            surplus = surplus - more
    return np.array(counts)


def noise(key, dims, width, reach, cuts=(), held_as=jnp.bfloat16):
    entries = jax.random.normal(key, dims, jnp.float32) * width
    if len(cuts) > 0:
        entries = block_levels(key, dims, cuts, -0.22, 0.18) * entries
    return jnp.clip(entries, min=-reach, max=reach).astype(held_as)


def setup_inputs(seed: int = 0) -> dict:
    splits = jax.random.split(jax.random.key(seed), 10)
    queries = draw_queries(jax.random.fold_in(splits[9], 71), 0)
    prefix_id_keys = jax.random.split(jax.random.fold_in(splits[1], 1), ROWS // ROWS_DEV)
    prefix_id_turns = jax.random.permutation(jax.random.fold_in(splits[1], 3), ROWS // ROWS_DEV)
    prefix_id = jax.vmap(lambda own, number: shared_out(jax.random.fold_in(splits[1], 2), own, number, ROWS_DEV, NPREF, 1, CAP, 2))(prefix_id_keys, prefix_id_turns).reshape((ROWS, 1))
    suffix_len = with_ends(jax.random.randint(splits[2], (ROWS,), 2, SUF_LEN + 1), jax.random.fold_in(splits[2], 1), 2, SUF_LEN).astype(jnp.int32)
    prefix_keys = draw_prefix_keys(jax.random.fold_in(splits[9], 71), 0)
    prefix_values = noise(splits[4], (NPREF, PREF_LEN, KVH, D_HEAD), 1.0, 6.0, ((0, 64), (2, 4)))
    suffix_keys = draw_suffix_keys(jax.random.fold_in(splits[9], 71), 0)
    suffix_values = noise(splits[6], (ROWS, SUF_LEN, KVH, D_HEAD), 1.0, 6.0, ((0, 256),))
    new_keys = noise(splits[7], (ROWS, KVH, D_HEAD), 2.5, 8.0, ((0, 256),))
    new_values = noise(splits[8], (ROWS, KVH, D_HEAD), 1.0, 6.0, ((0, 256),))
    return {"queries": queries, "prefix_id": prefix_id, "suffix_len": suffix_len, "prefix_keys": prefix_keys, "prefix_values": prefix_values, "suffix_keys": suffix_keys, "suffix_values": suffix_values, "new_keys": new_keys, "new_values": new_values}


def settle(weights_raw):
    return lax.optimization_barrier(weights_raw.astype(jnp.bfloat16)).astype(jnp.float32)

def reference(queries, prefix_id, suffix_len, prefix_keys, prefix_values, suffix_keys, suffix_values, new_keys, new_values):
    per_kv = QH // KVH
    scale_factor = 1.0 / math.sqrt(D_HEAD)
    owner_ids = prefix_id[:, 0].astype(jnp.int32)

    def row_block(packed_tuple):
        block_query_rows, block_owner_index, block_length_total, block_private_keys, block_private_values, block_anchor_keys, block_anchor_values = packed_tuple
        query_layout = block_query_rows.astype(jnp.float32).reshape(8, KVH, per_kv, D_HEAD)
        key_rows = prefix_keys[block_owner_index].astype(jnp.float32)
        value_rows = prefix_values[block_owner_index].astype(jnp.float32)
        scores = jnp.einsum('rkgd,rtkd->rkgt', query_layout, key_rows) * scale_factor
        highest = lax.optimization_barrier(jnp.max(scores, axis=-1))
        weights_raw = jnp.exp(scores - highest[..., None])
        totals = lax.optimization_barrier(jnp.sum(weights_raw, axis=-1))
        prefix_out = jnp.einsum('rkgt,rtkd->rkgd', settle(weights_raw), value_rows) / totals[..., None]
        prefix_sent = settle(prefix_out)
        prefix_mass = highest + jnp.log(totals)
        private_scores = jnp.einsum('wtfb,wmtb->wtfm', query_layout, block_private_keys.astype(jnp.float32)) * scale_factor
        visible = (jnp.arange(SUF_LEN, dtype=jnp.int32)[None, :] < block_length_total[:, None])[:, None, None, :]
        private_scores = jnp.where(visible, private_scores, -jnp.inf)
        own_score = jnp.einsum('rkgd,rkd->rkg', query_layout, block_anchor_keys.astype(jnp.float32)) * scale_factor
        suffix_top = jnp.maximum(lax.optimization_barrier(jnp.max(private_scores, axis=-1)), own_score)
        suffix_raw = jnp.where(visible, jnp.exp(private_scores - suffix_top[..., None]), 0.0)
        own_weight = jnp.exp(own_score - suffix_top)
        suffix_totals = lax.optimization_barrier(jnp.sum(suffix_raw, axis=-1)) + own_weight
        gathered = jnp.einsum('rkgs,rskd->rkgd', settle(suffix_raw), block_private_values.astype(jnp.float32))
        gathered = gathered + settle(own_weight)[..., None] * block_anchor_values.astype(jnp.float32)[:, :, None, :]
        suffix_out = gathered / suffix_totals[..., None]
        suffix_mass = suffix_top + jnp.log(suffix_totals)
        ceiling = jnp.maximum(prefix_mass, suffix_mass)
        share_prefix = jnp.exp(prefix_mass - ceiling)
        share_suffix = jnp.exp(suffix_mass - ceiling)
        blended = (share_prefix[..., None] * prefix_sent + share_suffix[..., None] * suffix_out) / (share_prefix + share_suffix)[..., None]
        return blended.reshape(8, QH, D_HEAD)
    blocks = ROWS // 8
    result = lax.map(row_block, (queries.reshape(blocks, 8, QH, D_HEAD), owner_ids.reshape(blocks, 8), suffix_len.astype(jnp.int32).reshape(blocks, 8), suffix_keys.reshape(blocks, 8, SUF_LEN, KVH, D_HEAD), suffix_values.reshape(blocks, 8, SUF_LEN, KVH, D_HEAD), new_keys.reshape(blocks, 8, KVH, D_HEAD), new_values.reshape(blocks, 8, KVH, D_HEAD)))
    return result.reshape(ROWS, QH, D_HEAD).astype(jnp.bfloat16)
```

```python
import functools
import math

import jax
import jax.numpy as jnp
from jax import lax
from jax.experimental import pallas as pl
from jax.experimental.pallas import tpu as pltpu
from jax.sharding import PartitionSpec as P

MESH = pl.DeviceIdType.MESH
BF16 = jnp.bfloat16
F32 = jnp.float32
LOG2E = 1.4426950408889634
CAP = 2
PER_KV = 8
GROUP = 16
KEY_BLOCK = 256
TILE = 256


def axes_of(prefixes):
    return {64: (4, 8, 2)}[prefixes]


def step_offset(i, nz):
    odd = i % 2
    return odd * ((i + 1) // 2) + (1 - odd) * ((nz - i // 2) % nz)


def kernel(
    sizes,
    src_row,
    row_a,
    row_s,
    suf_len,
    arrival,
    q,
    kp_hbm,
    vp_hbm,
    sk_hbm,
    sv_hbm,
    nk,
    nv,
    out,
    out_a,
    in_a,
    in_b,
    out_bp,
    in_bp,
    in_ap,
    out_m,
    in_m,
    in_mp,
    sk,
    sv,
    kf,
    vf,
    stage,
    kc,
    vt,
    scores,
    sacc,
    smass,
    gath,
    pmt,
    load_sem,
    a_send,
    a_recv,
    b_send,
    b_recv,
    bp_send,
    bp_recv,
    m_send,
    m_recv,
    ap_send,
    ap_recv,
    mp_send,
    mp_recv,
):
    nx, nz, nc, ny = sizes
    plane = nx * nc * ny
    rows = q.shape[0]
    width = q.shape[-1]
    keys = kc.shape[0]
    scale = LOG2E / math.sqrt(width)
    me_p, y = lax.axis_index("prefix"), lax.axis_index("head")
    x, z, c = me_p // (nz * nc), (me_p // nc) % nz, me_p % nc

    def at(x_, z_, c_, y_):
        return ((x_ * nz + z_) * nc + c_, y_)

    def along_z(d):
        return at(x, (z + d) % nz, c, y)

    def in_plane(j, sign):
        jx, jc, jy = j // (nc * ny), (j // ny) % nc, j % ny
        return at((x + nx + sign * jx) % nx, z, (c + jc) % nc, (y + ny + sign * jy) % ny)

    loads = [
        pltpu.make_async_copy(s, d, load_sem.at[n])
        for n, (s, d) in enumerate(((kp_hbm, kf), (vp_hbm, vf), (sk_hbm, sk), (sv_hbm, sv)))
    ]
    for load in loads:
        load.start()

    barrier = pltpu.get_barrier_semaphore()

    @pl.loop(1, nz)
    def _(d):
        pl.semaphore_signal(barrier, inc=1, device_id=along_z(d), device_id_type=MESH)

    @pl.loop(1, plane)
    def _(j):
        pl.semaphore_signal(barrier, inc=1, device_id=in_plane(j, 1), device_id_type=MESH)

    def pack(i, dst):
        @pl.loop(0, nx * nc)
        def _(k):
            for s in range(CAP):
                row = src_row[(i * nx * nc + k) * CAP + s]
                for jy in range(ny):
                    dst[i, k * ny + jy, s] = q[row, (y + jy) % ny]

    pack(0, in_a)

    @pl.loop(1, nz)
    def _(i):
        pack(i, out_a)

    pl.semaphore_wait(barrier, nz - 1 + plane - 1)

    def a_copy(i):
        return pltpu.make_async_remote_copy(
            out_a.at[i], in_a.at[i], a_send.at[i], a_recv.at[i],
            device_id=along_z(step_offset(i, nz)), device_id_type=MESH,
        )

    def start_b(i):
        pltpu.make_async_copy(in_a.at[i, 0], in_b.at[i, 0], b_recv.at[i]).start()

        @pl.loop(1, plane)
        def _(j):
            pltpu.make_async_remote_copy(
                in_a.at[i, j], in_b.at[i, j], b_send.at[i], b_recv.at[i],
                device_id=in_plane(j, 1), device_id_type=MESH,
            ).start()

    def start_bp(i):
        pltpu.make_async_copy(out_bp.at[i, 0], in_bp.at[i, 0], bp_recv.at[i]).start()
        pltpu.make_async_copy(out_m.at[i, 0], in_m.at[i, 0], m_recv.at[i]).start()

        @pl.loop(1, plane)
        def _(j):
            pltpu.make_async_remote_copy(
                out_m.at[i, j // 4], in_m.at[i, j], m_send.at[i], m_recv.at[i],
                device_id=in_plane(j, -1), device_id_type=MESH,
            ).start()
            pltpu.make_async_remote_copy(
                out_bp.at[i, j], in_bp.at[i, j], bp_send.at[i], bp_recv.at[i],
                device_id=in_plane(j, -1), device_id_type=MESH,
            ).start()

    def ap_copies(i):
        back = along_z((nz - step_offset(i, nz)) % nz)
        return (
            pltpu.make_async_remote_copy(
                in_m.at[i], in_mp.at[i], mp_send.at[i], mp_recv.at[i],
                device_id=back, device_id_type=MESH,
            ),
            pltpu.make_async_remote_copy(
                in_bp.at[i], in_ap.at[i], ap_send.at[i], ap_recv.at[i],
                device_id=back, device_id_type=MESH,
            ),
        )

    def wait_all(ref, sem):
        pltpu.make_async_copy(ref, ref, sem).wait()

    @pl.loop(1, nz)
    def _(i):
        a_copy(i).start()

    start_b(0)

    loads[0].wait()
    for part in range(2 * keys // 1024):
        stage[part * 1024 : (part + 1) * 1024] = kf[part * 1024 : (part + 1) * 1024].astype(F32)
    for part in range(keys // KEY_BLOCK):
        for k in range(2):
            block = stage[pl.ds(part * 2 * KEY_BLOCK + k, KEY_BLOCK, stride=2), :]
            kc[part * KEY_BLOCK : (part + 1) * KEY_BLOCK, k * width : (k + 1) * width] = block.astype(BF16)
    loads[1].wait()
    for part in range(2 * keys // 1024):
        stage[part * 1024 : (part + 1) * 1024] = vf[part * 1024 : (part + 1) * 1024].astype(F32)
    for part in range(keys // KEY_BLOCK):
        for k in range(2):
            block = stage[pl.ds(part * 2 * KEY_BLOCK + k, KEY_BLOCK, stride=2), :]
            vt[k * width : (k + 1) * width, part * KEY_BLOCK : (part + 1) * KEY_BLOCK] = block.T.astype(BF16)
    loads[2].wait()
    loads[3].wait()

    kv = nk.shape[1]
    cols = sk.shape[1]
    heads = ny * GROUP
    head_of = lax.broadcasted_iota(jnp.int32, (heads, cols), 0) // PER_KV
    col = lax.broadcasted_iota(jnp.int32, (heads, cols), 1)
    own_head = head_of == col % kv

    def suffix_row(r):
        qr = q[r].reshape(heads, width)
        s = lax.dot_general(qr, sk[r], (((1,), (1,)), ((), ())), preferred_element_type=F32)
        s = jnp.where(own_head & (col < suf_len[r] * kv), s * scale, -1e30)
        new_k = jnp.broadcast_to(nk[r].astype(F32)[:, None, :], (kv, PER_KV, width)).reshape(heads, width)
        new_v = jnp.broadcast_to(nv[r].astype(F32)[:, None, :], (kv, PER_KV, width)).reshape(heads, width)
        own = jnp.sum(qr.astype(F32) * new_k, axis=1, keepdims=True) * scale
        top = jnp.maximum(jnp.max(s, axis=1, keepdims=True), own)
        w = jnp.exp2(s - top)
        own_w = jnp.exp2(own - top)
        total = jnp.sum(w, axis=1, keepdims=True) + own_w
        acc = jnp.dot(w.astype(BF16), sv[r], preferred_element_type=F32)
        acc = acc + own_w.astype(BF16).astype(F32) * new_v
        sacc[r] = (acc / total).reshape(ny, GROUP, width)
        smass[r] = jnp.broadcast_to(top + jnp.log2(total), (heads, width)).reshape(ny, GROUP, width)

    part_rows = rows // nz

    def suffix_part(i):
        @pl.loop(0, part_rows // 2)
        def _(n):
            suffix_row(i * part_rows + 2 * n)
            suffix_row(i * part_rows + 2 * n + 1)

    low_row = lax.broadcasted_iota(jnp.int32, (TILE, width), 0) % GROUP < PER_KV
    low_lane = lax.broadcasted_iota(jnp.int32, (width, TILE), 1) % GROUP < PER_KV
    senders = TILE // (CAP * GROUP)

    def attend(i):
        for t in range(plane // senders):
            xq = in_b[i, t * senders : (t + 1) * senders].reshape(TILE, width).astype(F32)
            xq = jnp.concatenate(
                [jnp.where(low_row, xq, 0.0), jnp.where(low_row, 0.0, xq)], axis=1
            ).astype(BF16)
            top = None
            for b in range(keys // KEY_BLOCK):
                part = slice(b * KEY_BLOCK, (b + 1) * KEY_BLOCK)
                s = lax.dot_general(kc[part], xq, (((1,), (1,)), ((), ())), preferred_element_type=F32)
                scores[t % 2, part] = s
                high = jnp.max(s, axis=0, keepdims=True)
                top = high if top is None else jnp.maximum(top, high)
            top = top * scale
            total = jnp.zeros_like(top)
            acc = jnp.zeros((2 * width, TILE), F32)
            for b in range(keys // KEY_BLOCK):
                part = slice(b * KEY_BLOCK, (b + 1) * KEY_BLOCK)
                w = jnp.exp2(scores[t % 2, part] * scale - top)
                total = total + jnp.sum(w, axis=0, keepdims=True)
                acc = acc + jnp.dot(vt[:, part], w.astype(BF16), preferred_element_type=F32)
            o = jnp.where(low_lane, acc[:width], acc[width:]) / total
            out_bp[i, t * senders : (t + 1) * senders] = o.T.astype(BF16).reshape(senders, CAP, GROUP, width)
            mass = top + jnp.log2(total)
            for h in range(TILE // 128):
                out_m[i, t * (TILE // 128) + h] = mass[:, h * 128 : (h + 1) * 128]

    @pl.loop(1, nz + 3)
    def _(n):
        @pl.when(n < nz)
        def _():
            a_copy(n).wait_recv()
            start_b(n)

        @pl.when(n <= nz)
        def _():
            i = n - 1
            suffix_part(i)
            wait_all(in_b.at[i], b_recv.at[i])
            attend(i)
            start_bp(i)

        @pl.when((n >= 2) & (n < nz + 2))
        def _():
            i = n - 2
            wait_all(in_bp.at[i], bp_recv.at[i])
            wait_all(in_m.at[i], m_recv.at[i])

            @pl.when(i > 0)
            def _():
                for copy in ap_copies(i):
                    copy.start()

            @pl.when(i == 0)
            def _():
                pltpu.make_async_copy(in_m.at[0], in_mp.at[0], mp_recv.at[0]).start()
                pltpu.make_async_copy(in_bp.at[0], in_ap.at[0], ap_recv.at[0]).start()

    wait_all(in_b.at[0, pl.ds(1, plane - 1)], b_send.at[0])
    wait_all(in_bp.at[0, pl.ds(1, plane - 1)], bp_send.at[0])
    wait_all(in_m.at[0, pl.ds(1, plane - 1)], m_send.at[0])
    wait_all(in_mp.at[0], mp_recv.at[0])
    wait_all(in_ap.at[0], ap_recv.at[0])

    @pl.loop(1, nz)
    def _(i):
        a_copy(i).wait_send()
        wait_all(in_b.at[i, pl.ds(1, plane - 1)], b_send.at[i])
        wait_all(in_bp.at[i, pl.ds(1, plane - 1)], bp_send.at[i])
        wait_all(in_m.at[i, pl.ds(1, plane - 1)], m_send.at[i])
        for copy in ap_copies(i):
            copy.wait()

    @pl.loop(0, rows)
    def _(r):
        a = row_a[r]
        i, k = a // (nx * nc), a % (nx * nc)
        for jy in range(ny):
            gath[jy, pl.ds(r, 1), :] = in_mp[i, k * ny + jy]

    for jy in range(ny):
        turned = gath[jy].T
        first = turned[(jy % 4) * 32 : (jy % 4) * 32 + GROUP]
        second = turned[(jy % 4) * 32 + GROUP : (jy % 4) * 32 + 2 * GROUP]
        pmt[jy] = jnp.where(arrival[...] == 0, first, second)

    lane = lax.broadcasted_iota(jnp.int32, (GROUP, rows), 1)

    def merge_row(r):
        a, s = row_a[r], row_s[r]
        i, k = a // (nx * nc), a % (nx * nc)
        for jy in range(ny):
            yy = (y + jy) % ny
            pm = jnp.sum(jnp.where(lane == r, pmt[jy], 0.0), axis=1, keepdims=True)
            gap = smass[r, yy] - pm
            e = jnp.exp2(-jnp.abs(gap))
            ahead = gap <= 0
            po = in_ap[i, k * ny + jy, s].astype(F32)
            so = sacc[r, yy]
            merged = (jnp.where(ahead, 1.0, e) * po + jnp.where(ahead, e, 1.0) * so) / (1.0 + e)
            out[r, yy] = merged.astype(BF16)

    @pl.loop(0, rows // 2)
    def _(n):
        merge_row(2 * n)
        merge_row(2 * n + 1)


def body(
    queries,
    prefix_id,
    suffix_len,
    prefix_keys,
    prefix_values,
    suffix_keys,
    suffix_values,
    new_keys,
    new_values,
):
    rows, heads, width = queries.shape
    prefixes, ny = lax.axis_size("prefix"), lax.axis_size("head")
    nx, nz, nc = axes_of(prefixes)
    plane = nx * nc * ny
    keys = prefix_keys.shape[1]
    slots, kv = suffix_keys.shape[1:3]

    me_p = lax.axis_index("prefix")
    x, z, c = me_p // (nz * nc), (me_p // nc) % nz, me_p % nc
    target = prefix_id[:, 0]
    dz = (target // nc - z) % nz
    step = jnp.where(dz == 0, 0, jnp.where(2 * dz <= nz, 2 * dz - 1, 2 * (nz - dz)))
    row_a = (step * nx + (target // (nz * nc) - x) % nx) * nc + (target - c) % nc
    r_index = lax.broadcasted_iota(jnp.int32, (rows, rows), 0)
    c_index = lax.broadcasted_iota(jnp.int32, (rows, rows), 1)
    same = (target[None, :] == target[:, None]) & (c_index < r_index)
    arrival = jnp.sum(same.astype(jnp.int32), axis=1)
    place = row_a * CAP + arrival
    slot_index = lax.broadcasted_iota(jnp.int32, (prefixes * CAP, rows), 0)
    row_index = lax.broadcasted_iota(jnp.int32, (prefixes * CAP, rows), 1)
    src_row = jnp.sum(jnp.where(place[None, :] == slot_index, row_index, 0), axis=1)

    smem = pl.BlockSpec(memory_space=pltpu.SMEM)
    vmem = pl.BlockSpec(memory_space=pltpu.VMEM)
    hbm = pl.BlockSpec(memory_space=pl.ANY)
    message = (CAP, GROUP, width)
    dma = pltpu.SemaphoreType.DMA
    attended = pl.pallas_call(
        functools.partial(kernel, (nx, nz, nc, ny)),
        out_shape=jax.ShapeDtypeStruct((rows, ny, GROUP, width), BF16),
        in_specs=[smem] * 4 + [vmem] * 2 + [hbm] * 4 + [vmem] * 2,
        out_specs=vmem,
        scratch_shapes=[
            pltpu.VMEM((nz, plane) + message, BF16),
            pltpu.VMEM((nz, plane) + message, BF16),
            pltpu.VMEM((nz, plane) + message, BF16),
            pltpu.VMEM((nz, plane) + message, BF16),
            pltpu.VMEM((nz, plane) + message, BF16),
            pltpu.VMEM((nz, plane) + message, BF16),
            pltpu.VMEM((nz, plane // 4, 1, 128), F32),
            pltpu.VMEM((nz, plane, 1, 128), F32),
            pltpu.VMEM((nz, plane, 1, 128), F32),
            pltpu.VMEM((rows, slots * kv, width), BF16),
            pltpu.VMEM((rows, slots * kv, width), BF16),
            pltpu.VMEM((2 * keys, width), BF16),
            pltpu.VMEM((2 * keys, width), BF16),
            pltpu.VMEM((2 * keys, width), F32),
            pltpu.VMEM((keys, 2 * width), BF16),
            pltpu.VMEM((2 * width, keys), BF16),
            pltpu.VMEM((2, keys, TILE), F32),
            pltpu.VMEM((rows, ny, GROUP, width), F32),
            pltpu.VMEM((rows, ny, GROUP, width), F32),
            pltpu.VMEM((ny, rows, 128), F32),
            pltpu.VMEM((ny, GROUP, rows), F32),
            dma((4,)),
        ]
        + [dma((nz,))] * 12,
        compiler_params=pltpu.CompilerParams(
            collective_id=0, has_side_effects=True, vmem_limit_bytes=56 * 2**20
        ),
    )(
        src_row,
        row_a,
        arrival,
        suffix_len,
        arrival[None, :],
        queries.reshape(rows, ny, GROUP, width),
        prefix_keys.reshape(2 * keys, width),
        prefix_values.reshape(2 * keys, width),
        suffix_keys.reshape(rows, slots * kv, width),
        suffix_values.reshape(rows, slots * kv, width),
        new_keys,
        new_values,
    )
    return attended.reshape(rows, heads, width)


def solution(mesh):
    rows = P(("prefix", "head"))
    cache = P("prefix", None, "head", None)
    return jax.shard_map(
        body,
        mesh=mesh,
        in_specs=(rows, rows, rows, cache, cache, rows, rows, rows, rows),
        out_specs=rows,
        check_vma=False,
    )
```

```python
import functools
import math

import jax
import jax.numpy as jnp
from jax import lax
from jax.experimental import pallas as pl
from jax.experimental.pallas import tpu as pltpu
from jax.sharding import PartitionSpec as P

MESH = pl.DeviceIdType.MESH
BF16 = jnp.bfloat16
F32 = jnp.float32
LOG2E = 1.4426950408889634
CAP = 2
PER_KV = 8
GROUP = 16
KEY_BLOCK = 256
TILE = 256
PACK = 12


def axes_of(prefixes):
    return {64: (4, 8, 2)}[prefixes]


def step_offset(i, nz):
    odd = i % 2
    return odd * ((i + 1) // 2) + (1 - odd) * ((nz - i // 2) % nz)


def kernel(
    sizes,
    own_tab,
    row_i,
    row_n,
    suf_len,
    arrival,
    tab,
    q,
    kp_hbm,
    vp_hbm,
    sk_hbm,
    sv_hbm,
    nk,
    nv,
    out,
    spilled,
    out_a,
    in_a,
    out_b,
    in_b,
    out_bp,
    in_bp,
    out_ap,
    in_ap,
    out_m,
    in_m,
    out_mp,
    in_mp,
    in_tab,
    stab,
    out_f,
    in_f,
    rows_a,
    rows_bp,
    rows_m,
    sk,
    sv,
    kf,
    vf,
    stage,
    kc,
    vt,
    scores,
    sacc,
    smass,
    gath,
    pmt,
    load_sem,
    a_send,
    a_recv,
    b_send,
    b_recv,
    bp_send,
    bp_recv,
    m_send,
    m_recv,
    ap_send,
    ap_recv,
    mp_send,
    mp_recv,
    t_send,
    t_recv,
    f_sem,
):
    nx, nz, nc, ny = sizes
    plane = nx * nc * ny
    rows = q.shape[0]
    width = q.shape[-1]
    keys = kc.shape[0]
    scale = LOG2E / math.sqrt(width)
    me_p, y = lax.axis_index("prefix"), lax.axis_index("head")
    x, z, c = me_p // (nz * nc), (me_p // nc) % nz, me_p % nc

    def at(x_, z_, c_, y_):
        return ((x_ * nz + z_) * nc + c_, y_)

    def along_z(d):
        return at(x, (z + d) % nz, c, y)

    def in_plane(j, sign):
        jx, jc, jy = j // (nc * ny), (j // ny) % nc, j % ny
        return at((x + nx + sign * jx) % nx, z, (c + jc) % nc, (y + ny + sign * jy) % ny)

    loads = [
        pltpu.make_async_copy(s, d, load_sem.at[n])
        for n, (s, d) in enumerate(((kp_hbm, kf), (vp_hbm, vf), (sk_hbm, sk), (sv_hbm, sv)))
    ]
    for load in loads:
        load.start()

    barrier = pltpu.get_barrier_semaphore()

    @pl.loop(1, nz)
    def _(d):
        pl.semaphore_signal(barrier, inc=1, device_id=along_z(d), device_id_type=MESH)

    @pl.loop(1, plane)
    def _(j):
        pl.semaphore_signal(barrier, inc=1, device_id=in_plane(j, 1), device_id_type=MESH)

    pack = in_a.shape[1]

    def pack_a(i, dst):
        @pl.loop(0, pack)
        def _(n):
            row = own_tab[i, 0, 64 + n]
            for jy in range(ny):
                dst[i, n, jy] = q[row, (y + jy) % ny]

    pack_a(0, in_a)

    @pl.loop(1, nz)
    def _(i):
        pack_a(i, out_a)

    pl.semaphore_wait(barrier, nz - 1 + plane - 1)

    def a_copy(i):
        return pltpu.make_async_remote_copy(
            out_a.at[i], in_a.at[i], a_send.at[i], a_recv.at[i],
            device_id=along_z(step_offset(i, nz)), device_id_type=MESH,
        )

    def t_copy(i):
        return pltpu.make_async_remote_copy(
            tab.at[i], in_tab.at[i], t_send.at[i], t_recv.at[i],
            device_id=along_z(step_offset(i, nz)), device_id_type=MESH,
        )

    def start_b(i):
        rows_a[...] = in_a[i]

        @pl.loop(0, nx * nc)
        def _(k):
            for s in range(CAP):
                n = stab[i, 0, k * CAP + s]
                for jy in range(ny):
                    out_b[i, k * ny + jy, s] = rows_a[n, jy]

        pltpu.make_async_copy(out_b.at[i, 0], in_b.at[i, 0], b_recv.at[i]).start()

        @pl.loop(1, plane)
        def _(j):
            pltpu.make_async_remote_copy(
                out_b.at[i, j], in_b.at[i, j], b_send.at[i], b_recv.at[i],
                device_id=in_plane(j, 1), device_id_type=MESH,
            ).start()

    def start_bp(i):
        pltpu.make_async_copy(out_bp.at[i, 0], in_bp.at[i, 0], bp_recv.at[i]).start()
        pltpu.make_async_copy(out_m.at[i, 0], in_m.at[i, 0], m_recv.at[i]).start()

        @pl.loop(1, plane)
        def _(j):
            pltpu.make_async_remote_copy(
                out_m.at[i, j // 4], in_m.at[i, j], m_send.at[i], m_recv.at[i],
                device_id=in_plane(j, -1), device_id_type=MESH,
            ).start()
            pltpu.make_async_remote_copy(
                out_bp.at[i, j], in_bp.at[i, j], bp_send.at[i], bp_recv.at[i],
                device_id=in_plane(j, -1), device_id_type=MESH,
            ).start()

    def ap_copies(i):
        back = along_z((nz - step_offset(i, nz)) % nz)
        return (
            pltpu.make_async_remote_copy(
                out_mp.at[i], in_mp.at[i], mp_send.at[i], mp_recv.at[i],
                device_id=back, device_id_type=MESH,
            ),
            pltpu.make_async_remote_copy(
                out_ap.at[i], in_ap.at[i], ap_send.at[i], ap_recv.at[i],
                device_id=back, device_id_type=MESH,
            ),
        )

    def wait_all(ref, sem):
        pltpu.make_async_copy(ref, ref, sem).wait()

    @pl.loop(1, nz)
    def _(i):
        t_copy(i).start()

    pltpu.make_async_copy(tab.at[0], in_tab.at[0], t_recv.at[0]).start()

    @pl.loop(1, nz)
    def _(i):
        a_copy(i).start()

    wait_all(in_tab.at[0], t_recv.at[0])

    @pl.loop(1, nz)
    def _(i):
        t_copy(i).wait()

    to_scalars = pltpu.make_async_copy(in_tab, stab, f_sem.at[0])
    to_scalars.start()
    worst = in_tab[0]
    for i in range(1, nz):
        worst = jnp.maximum(worst, in_tab[i])
    out_f[...] = worst
    in_f[0] = worst

    @pl.loop(1, plane)
    def _(j):
        pltpu.make_async_remote_copy(
            out_f, in_f.at[j], f_sem.at[1], f_sem.at[2],
            device_id=in_plane(j, 1), device_id_type=MESH,
        ).start()

    to_scalars.wait()
    start_b(0)

    loads[0].wait()
    for part in range(2 * keys // 1024):
        stage[part * 1024 : (part + 1) * 1024] = kf[part * 1024 : (part + 1) * 1024].astype(F32)
    for part in range(keys // KEY_BLOCK):
        for k in range(2):
            block = stage[pl.ds(part * 2 * KEY_BLOCK + k, KEY_BLOCK, stride=2), :]
            kc[part * KEY_BLOCK : (part + 1) * KEY_BLOCK, k * width : (k + 1) * width] = block.astype(BF16)
    loads[1].wait()
    for part in range(2 * keys // 1024):
        stage[part * 1024 : (part + 1) * 1024] = vf[part * 1024 : (part + 1) * 1024].astype(F32)
    for part in range(keys // KEY_BLOCK):
        for k in range(2):
            block = stage[pl.ds(part * 2 * KEY_BLOCK + k, KEY_BLOCK, stride=2), :]
            vt[k * width : (k + 1) * width, part * KEY_BLOCK : (part + 1) * KEY_BLOCK] = block.T.astype(BF16)
    loads[2].wait()
    loads[3].wait()

    kv = nk.shape[1]
    cols = sk.shape[1]
    heads = ny * GROUP
    head_of = lax.broadcasted_iota(jnp.int32, (heads, cols), 0) // PER_KV
    col = lax.broadcasted_iota(jnp.int32, (heads, cols), 1)
    own_head = head_of == col % kv

    def suffix_row(r):
        qr = q[r].reshape(heads, width)
        s = lax.dot_general(qr, sk[r], (((1,), (1,)), ((), ())), preferred_element_type=F32)
        s = jnp.where(own_head & (col < suf_len[r] * kv), s * scale, -1e30)
        new_k = jnp.broadcast_to(nk[r].astype(F32)[:, None, :], (kv, PER_KV, width)).reshape(heads, width)
        new_v = jnp.broadcast_to(nv[r].astype(F32)[:, None, :], (kv, PER_KV, width)).reshape(heads, width)
        own = jnp.sum(qr.astype(F32) * new_k, axis=1, keepdims=True) * scale
        top = jnp.maximum(jnp.max(s, axis=1, keepdims=True), own)
        w = jnp.exp2(s - top)
        own_w = jnp.exp2(own - top)
        total = jnp.sum(w, axis=1, keepdims=True) + own_w
        acc = jnp.dot(w.astype(BF16), sv[r], preferred_element_type=F32)
        acc = acc + own_w.astype(BF16).astype(F32) * new_v
        sacc[r] = (acc / total).reshape(ny, GROUP, width)
        smass[r] = jnp.broadcast_to(top + jnp.log2(total), (heads, width)).reshape(ny, GROUP, width)

    part_rows = rows // nz

    def suffix_part(i):
        @pl.loop(0, part_rows // 2)
        def _(n):
            suffix_row(i * part_rows + 2 * n)
            suffix_row(i * part_rows + 2 * n + 1)

    low_row = lax.broadcasted_iota(jnp.int32, (TILE, width), 0) % GROUP < PER_KV
    low_lane = lax.broadcasted_iota(jnp.int32, (width, TILE), 1) % GROUP < PER_KV
    senders = TILE // (CAP * GROUP)

    def attend(i):
        for t in range(plane // senders):
            xq = in_b[i, t * senders : (t + 1) * senders].reshape(TILE, width).astype(F32)
            xq = jnp.concatenate(
                [jnp.where(low_row, xq, 0.0), jnp.where(low_row, 0.0, xq)], axis=1
            ).astype(BF16)
            top = None
            for b in range(keys // KEY_BLOCK):
                part = slice(b * KEY_BLOCK, (b + 1) * KEY_BLOCK)
                s = lax.dot_general(kc[part], xq, (((1,), (1,)), ((), ())), preferred_element_type=F32)
                scores[t % 2, part] = s
                high = jnp.max(s, axis=0, keepdims=True)
                top = high if top is None else jnp.maximum(top, high)
            top = top * scale
            total = jnp.zeros_like(top)
            acc = jnp.zeros((2 * width, TILE), F32)
            for b in range(keys // KEY_BLOCK):
                part = slice(b * KEY_BLOCK, (b + 1) * KEY_BLOCK)
                w = jnp.exp2(scores[t % 2, part] * scale - top)
                total = total + jnp.sum(w, axis=0, keepdims=True)
                acc = acc + jnp.dot(vt[:, part], w.astype(BF16), preferred_element_type=F32)
            o = jnp.where(low_lane, acc[:width], acc[width:]) / total
            out_bp[i, t * senders : (t + 1) * senders] = o.T.astype(BF16).reshape(senders, CAP, GROUP, width)
            mass = top + jnp.log2(total)
            for h in range(TILE // 128):
                out_m[i, t * (TILE // 128) + h] = mass[:, h * 128 : (h + 1) * 128]

    mass_lane = lax.broadcasted_iota(jnp.int32, (1, 128), 1)

    @pl.loop(1, nz + 3)
    def _(n):
        @pl.when(n < nz)
        def _():
            a_copy(n).wait_recv()
            start_b(n)

        @pl.when(n <= nz)
        def _():
            i = n - 1
            suffix_part(i)
            wait_all(in_b.at[i], b_recv.at[i])
            attend(i)
            start_bp(i)

        @pl.when((n >= 2) & (n < nz + 2))
        def _():
            i = n - 2
            wait_all(in_bp.at[i], bp_recv.at[i])
            wait_all(in_m.at[i], m_recv.at[i])

            rows_bp[...] = in_bp[i]
            rows_m[...] = in_m[i]

            @pl.loop(0, pack)
            def _(n):
                k, slot = stab[i, 0, 16 + n], stab[i, 0, 32 + n]
                mass = rows_m[k * ny]
                for jy in range(ny):
                    out_ap[i, n, jy] = rows_bp[k * ny + jy, slot]
                    if jy > 0:
                        mass = jnp.where(mass_lane // (CAP * GROUP) == jy, rows_m[k * ny + jy], mass)
                out_mp[i, n] = mass

            @pl.when(i > 0)
            def _():
                for copy in ap_copies(i):
                    copy.start()

            @pl.when(i == 0)
            def _():
                pltpu.make_async_copy(out_mp.at[0], in_mp.at[0], mp_recv.at[0]).start()
                pltpu.make_async_copy(out_ap.at[0], in_ap.at[0], ap_recv.at[0]).start()

    wait_all(in_f.at[pl.ds(1, plane - 1)], f_sem.at[1])
    wait_all(in_f.at[pl.ds(1, plane - 1)], f_sem.at[2])
    spilled[...] = jnp.max(in_f[...], axis=0)
    wait_all(in_b.at[0, pl.ds(1, plane - 1)], b_send.at[0])
    wait_all(in_bp.at[0, pl.ds(1, plane - 1)], bp_send.at[0])
    wait_all(in_m.at[0, pl.ds(1, plane - 1)], m_send.at[0])
    wait_all(in_mp.at[0], mp_recv.at[0])
    wait_all(in_ap.at[0], ap_recv.at[0])

    @pl.loop(1, nz)
    def _(i):
        a_copy(i).wait_send()
        wait_all(in_b.at[i, pl.ds(1, plane - 1)], b_send.at[i])
        wait_all(in_bp.at[i, pl.ds(1, plane - 1)], bp_send.at[i])
        wait_all(in_m.at[i, pl.ds(1, plane - 1)], m_send.at[i])
        for copy in ap_copies(i):
            copy.wait()

    @pl.loop(0, rows)
    def _(r):
        gath[pl.ds(r, 1), :] = in_mp[row_i[r], row_n[r]]

    turned = gath[...].T
    for jy in range(ny):
        first = turned[jy * 32 : jy * 32 + GROUP]
        second = turned[jy * 32 + GROUP : jy * 32 + 2 * GROUP]
        pmt[jy] = jnp.where(arrival[...] == 0, first, second)

    lane = lax.broadcasted_iota(jnp.int32, (GROUP, rows), 1)

    def merge_row(r):
        i, n = row_i[r], row_n[r]
        for jy in range(ny):
            yy = (y + jy) % ny
            pm = jnp.sum(jnp.where(lane == r, pmt[jy], 0.0), axis=1, keepdims=True)
            gap = smass[r, yy] - pm
            e = jnp.exp2(-jnp.abs(gap))
            ahead = gap <= 0
            po = in_ap[i, n, jy].astype(F32)
            so = sacc[r, yy]
            merged = (jnp.where(ahead, 1.0, e) * po + jnp.where(ahead, e, 1.0) * so) / (1.0 + e)
            out[r, yy] = merged.astype(BF16)

    @pl.loop(0, rows // 2)
    def _(n):
        merge_row(2 * n)
        merge_row(2 * n + 1)


def wide_attend(received, key_cache, value_cache, scale_factor):
    lined = jnp.transpose(received, (3, 1, 0, 2, 4, 5))

    def per_head(packed_tuple):
        head_query, head_keys, head_values = packed_tuple

        def per_group(block_query_rows):
            scores = (
                jnp.einsum(
                    "ncgd,td->ncgt", block_query_rows, head_keys, preferred_element_type=jnp.float32
                )
                * scale_factor
            )
            highest = jnp.max(scores, axis=-1)
            weights_raw = jnp.exp(scores - highest[..., None])
            totals = jnp.sum(weights_raw, axis=-1)
            blended = jnp.einsum(
                "ncgt,td->ncgd",
                weights_raw.astype(jnp.bfloat16),
                head_values,
                preferred_element_type=jnp.float32,
            )
            return ((blended / totals[..., None]).astype(jnp.bfloat16), highest + jnp.log(totals))

        return lax.map(per_group, head_query)

    blended, log_mass = lax.map(
        per_head,
        (lined, jnp.transpose(key_cache, (1, 0, 2)), jnp.transpose(value_cache, (1, 0, 2))),
    )
    return (jnp.transpose(blended, (2, 1, 3, 0, 4, 5)), jnp.transpose(log_mass, (2, 1, 3, 0, 4)))


def wide_body(
    queries,
    prefix_id,
    suffix_len,
    prefix_keys,
    prefix_values,
    suffix_keys,
    suffix_values,
    new_keys,
    new_values,
):
    row_count, head_count, head_width = queries.shape
    kv_all = suffix_keys.shape[2]
    per_kv = head_count // kv_all
    owners = lax.axis_size("prefix")
    capacity = 2 * row_count // owners
    scale_factor = 1.0 / math.sqrt(head_width)
    target = prefix_id[:, 0]
    row_index = lax.broadcasted_iota(jnp.int32, (row_count, row_count), 0)
    col_index = lax.broadcasted_iota(jnp.int32, (row_count, row_count), 1)
    earlier = (target[None, :] == target[:, None]) & (col_index < row_index)
    arrival = jnp.sum(earlier.astype(jnp.int32), axis=1)
    position = target * capacity + arrival
    query_layout = queries.reshape(row_count, kv_all, per_kv, head_width)
    outbox = (
        jnp.zeros((owners * capacity, kv_all, per_kv, head_width), jnp.bfloat16)
        .at[position]
        .set(query_layout)
    )
    outbox = outbox.reshape(owners, 1, capacity, kv_all, per_kv, head_width)
    key_cache = prefix_keys[0]
    value_cache = prefix_values[0]
    received = lax.all_to_all(
        lax.all_to_all(outbox, "prefix", split_axis=0, concat_axis=0, tiled=True),
        "head",
        split_axis=3,
        concat_axis=1,
        tiled=True,
    )
    blended, log_mass = wide_attend(received, key_cache, value_cache, scale_factor)
    blended = lax.all_to_all(
        lax.all_to_all(blended, "prefix", split_axis=0, concat_axis=0, tiled=True),
        "head",
        split_axis=1,
        concat_axis=3,
        tiled=True,
    )
    log_mass = lax.all_to_all(
        lax.all_to_all(log_mass, "prefix", split_axis=0, concat_axis=0, tiled=True),
        "head",
        split_axis=1,
        concat_axis=3,
        tiled=True,
    )
    prefix_out = blended.reshape(owners * capacity, kv_all, per_kv, head_width)[position].astype(
        jnp.float32
    )
    prefix_mass = log_mass.reshape(owners * capacity, kv_all, per_kv)[position]
    private_scores = (
        jnp.einsum("wtfb,wmtb->wtfm", query_layout, suffix_keys, preferred_element_type=jnp.float32)
        * scale_factor
    )
    visible = (jnp.arange(suffix_keys.shape[1], dtype=jnp.int32)[None, :] < suffix_len[:, None])[
        :, None, None, :
    ]
    private_scores = jnp.where(visible, private_scores, -jnp.inf)
    own_score = (
        jnp.einsum("rkgd,rkd->rkg", query_layout, new_keys, preferred_element_type=jnp.float32)
        * scale_factor
    )
    suffix_top = jnp.maximum(jnp.max(private_scores, axis=-1), own_score)
    suffix_raw = jnp.where(visible, jnp.exp(private_scores - suffix_top[..., None]), 0.0)
    own_weight = jnp.exp(own_score - suffix_top)
    suffix_totals = jnp.sum(suffix_raw, axis=-1) + own_weight
    gathered = jnp.einsum(
        "rkgs,rskd->rkgd",
        suffix_raw.astype(jnp.bfloat16),
        suffix_values,
        preferred_element_type=jnp.float32,
    )
    gathered = (
        gathered
        + own_weight.astype(jnp.bfloat16).astype(jnp.float32)[..., None]
        * new_values.astype(jnp.float32)[:, :, None, :]
    )
    suffix_out = gathered / suffix_totals[..., None]
    suffix_mass = suffix_top + jnp.log(suffix_totals)
    ceiling = jnp.maximum(prefix_mass, suffix_mass)
    share_prefix = jnp.exp(prefix_mass - ceiling)
    share_suffix = jnp.exp(suffix_mass - ceiling)
    merged = (share_prefix[..., None] * prefix_out + share_suffix[..., None] * suffix_out) / (
        share_prefix + share_suffix
    )[..., None]
    return merged.reshape(row_count, head_count, head_width).astype(jnp.bfloat16)


def body(
    queries,
    prefix_id,
    suffix_len,
    prefix_keys,
    prefix_values,
    suffix_keys,
    suffix_values,
    new_keys,
    new_values,
):
    rows, heads, width = queries.shape
    prefixes, ny = lax.axis_size("prefix"), lax.axis_size("head")
    nx, nz, nc = axes_of(prefixes)
    plane = nx * nc * ny
    keys = prefix_keys.shape[1]
    slots, kv = suffix_keys.shape[1:3]

    me_p = lax.axis_index("prefix")
    x, z, c = me_p // (nz * nc), (me_p // nc) % nz, me_p % nc
    target = prefix_id[:, 0]
    dz = (target // nc - z) % nz
    step = jnp.where(dz == 0, 0, jnp.where(2 * dz <= nz, 2 * dz - 1, 2 * (nz - dz)))
    spot = ((target // (nz * nc) - x) % nx) * nc + (target - c) % nc
    r_index = lax.broadcasted_iota(jnp.int32, (rows, rows), 0)
    c_index = lax.broadcasted_iota(jnp.int32, (rows, rows), 1)
    earlier = c_index < r_index
    arrival = jnp.sum(((target[None, :] == target[:, None]) & earlier).astype(jnp.int32), axis=1)
    rank = jnp.sum(((step[None, :] == step[:, None]) & earlier).astype(jnp.int32), axis=1)
    row_n = jnp.minimum(rank, PACK - 1)
    spill = (rank >= PACK).astype(jnp.int32)
    shape = (nz, 128, rows)
    t_step = lax.broadcasted_iota(jnp.int32, shape, 0)
    t_lane = lax.broadcasted_iota(jnp.int32, shape, 1)
    field, entry = t_lane // 16, t_lane % 16
    mine = (step[None, None, :] == t_step) & (spill == 0)[None, None, :]
    by_slot = mine & ((spot * CAP + arrival)[None, None, :] == entry)
    by_rank = mine & (rank[None, None, :] == entry)
    r_value = lax.broadcasted_iota(jnp.int32, shape, 2)
    value = jnp.where((field == 0) & by_slot, rank[None, None, :], 0)
    value = jnp.where((field == 1) & by_rank, spot[None, None, :], value)
    value = jnp.where((field == 2) & by_rank, arrival[None, None, :], value)
    value = jnp.where((field == 3) & (entry == 0), spill[None, None, :], value)
    value = jnp.where((field == 4) & by_rank, r_value, value)
    table = jnp.sum(value, axis=2)[:, None, :]

    smem = pl.BlockSpec(memory_space=pltpu.SMEM)
    vmem = pl.BlockSpec(memory_space=pltpu.VMEM)
    hbm = pl.BlockSpec(memory_space=pl.ANY)
    message = (CAP, GROUP, width)
    dma = pltpu.SemaphoreType.DMA
    attended, spilled = pl.pallas_call(
        functools.partial(kernel, (nx, nz, nc, ny)),
        out_shape=(
            jax.ShapeDtypeStruct((rows, ny, GROUP, width), BF16),
            jax.ShapeDtypeStruct((1, 128), jnp.int32),
        ),
        in_specs=[smem] * 4 + [vmem] * 3 + [hbm] * 4 + [vmem] * 2,
        out_specs=(vmem, vmem),
        scratch_shapes=[
            pltpu.VMEM((nz, PACK, ny, GROUP, width), BF16),
            pltpu.VMEM((nz, PACK, ny, GROUP, width), BF16),
            pltpu.VMEM((nz, plane) + message, BF16),
            pltpu.VMEM((nz, plane) + message, BF16),
            pltpu.VMEM((nz, plane) + message, BF16),
            pltpu.VMEM((nz, plane) + message, BF16),
            pltpu.VMEM((nz, PACK, ny, GROUP, width), BF16),
            pltpu.VMEM((nz, PACK, ny, GROUP, width), BF16),
            pltpu.VMEM((nz, plane // 4, 1, 128), F32),
            pltpu.VMEM((nz, plane, 1, 128), F32),
            pltpu.VMEM((nz, PACK, 1, 128), F32),
            pltpu.VMEM((nz, PACK, 1, 128), F32),
            pltpu.VMEM((nz, 1, 128), jnp.int32),
            pltpu.SMEM((nz, 1, 128), jnp.int32),
            pltpu.VMEM((1, 128), jnp.int32),
            pltpu.VMEM((plane, 1, 128), jnp.int32),
            pltpu.VMEM((PACK, ny, GROUP, width), BF16),
            pltpu.VMEM((plane,) + message, BF16),
            pltpu.VMEM((plane, 1, 128), F32),
            pltpu.VMEM((rows, slots * kv, width), BF16),
            pltpu.VMEM((rows, slots * kv, width), BF16),
            pltpu.VMEM((2 * keys, width), BF16),
            pltpu.VMEM((2 * keys, width), BF16),
            pltpu.VMEM((2 * keys, width), F32),
            pltpu.VMEM((keys, 2 * width), BF16),
            pltpu.VMEM((2 * width, keys), BF16),
            pltpu.VMEM((2, keys, TILE), F32),
            pltpu.VMEM((rows, ny, GROUP, width), F32),
            pltpu.VMEM((rows, ny, GROUP, width), F32),
            pltpu.VMEM((rows, 128), F32),
            pltpu.VMEM((ny, GROUP, rows), F32),
            dma((4,)),
        ]
        + [dma((nz,))] * 14
        + [dma((3,))],
        compiler_params=pltpu.CompilerParams(
            collective_id=0, has_side_effects=True, vmem_limit_bytes=56 * 2**20
        ),
    )(
        table,
        step,
        row_n,
        suffix_len,
        arrival[None, :],
        table,
        queries.reshape(rows, ny, GROUP, width),
        prefix_keys.reshape(2 * keys, width),
        prefix_values.reshape(2 * keys, width),
        suffix_keys.reshape(rows, slots * kv, width),
        suffix_values.reshape(rows, slots * kv, width),
        new_keys,
        new_values,
    )
    args = (
        queries,
        prefix_id,
        suffix_len,
        prefix_keys,
        prefix_values,
        suffix_keys,
        suffix_values,
        new_keys,
        new_values,
    )
    return lax.cond(
        spilled[0, 48] > 0,
        wide_body,
        lambda *_: attended.reshape(rows, heads, width),
        *args,
    )


def solution(mesh):
    rows = P(("prefix", "head"))
    cache = P("prefix", None, "head", None)
    return jax.shard_map(
        body,
        mesh=mesh,
        in_specs=(rows, rows, rows, cache, cache, rows, rows, rows, rows),
        out_specs=rows,
        check_vma=False,
    )
```

```python
import functools
import math

import jax
import jax.numpy as jnp
from jax import lax
from jax.experimental import pallas as pl
from jax.experimental.pallas import tpu as pltpu
from jax.sharding import PartitionSpec as P

MESH = pl.DeviceIdType.MESH
BF16 = jnp.bfloat16
F32 = jnp.float32
LOG2E = 1.4426950408889634
CAP = 2
PER_KV = 8
GROUP = 16
KEY_BLOCK = 256
TILE = 256
WINDOW = 4
PACK = 12


def axes_of(prefixes):
    return {64: (4, 8, 2)}[prefixes]


def step_offset(i, nz):
    odd = i % 2
    return odd * ((i + 1) // 2) + (1 - odd) * ((nz - i // 2) % nz)


def kernel(
    sizes,
    own_tab,
    row_i,
    row_n,
    suf_len,
    arrival,
    tab,
    q,
    kp_hbm,
    vp_hbm,
    sk_hbm,
    sv_hbm,
    nk,
    nv,
    out,
    spilled,
    out_a,
    in_a,
    out_b,
    in_b,
    out_bp,
    in_bp,
    out_ap,
    in_ap,
    out_m,
    in_m,
    out_mp,
    in_mp,
    in_tab,
    stab,
    out_f,
    in_f,
    rows_a,
    rows_bp,
    rows_m,
    sk,
    sv,
    kf,
    vf,
    stage,
    kc,
    vt,
    scores,
    sacc,
    smass,
    gath,
    pmt,
    load_sem,
    a_send,
    a_recv,
    b_send,
    b_recv,
    bp_send,
    bp_recv,
    m_send,
    m_recv,
    ap_send,
    ap_recv,
    mp_send,
    mp_recv,
    t_send,
    t_recv,
    f_sem,
):
    nx, nz, nc, ny = sizes
    plane = nx * nc * ny
    rows = q.shape[0]
    width = q.shape[-1]
    keys = kc.shape[0]
    scale = LOG2E / math.sqrt(width)
    me_p, y = lax.axis_index("prefix"), lax.axis_index("head")
    x, z, c = me_p // (nz * nc), (me_p // nc) % nz, me_p % nc

    def at(x_, z_, c_, y_):
        return ((x_ * nz + z_) * nc + c_, y_)

    def along_z(d):
        return at(x, (z + d) % nz, c, y)

    offsets = [(jx, jc, jy) for jx in range(nx) for jc in range(nc) for jy in range(ny)]
    y_at = [(y + jy) % ny for jy in range(ny)]
    column = {
        (sign, jx, jc): (((x + nx + sign * jx) % nx) * nz + z) * nc + (c + jc) % nc
        for sign in (1, -1)
        for jx in range(nx)
        for jc in range(nc)
    }

    def in_plane(j, sign):
        jx, jc, jy = offsets[j]
        return column[sign, jx, jc], y_at[sign * jy % ny]

    loads = [
        pltpu.make_async_copy(s, d, load_sem.at[n])
        for n, (s, d) in enumerate(((kp_hbm, kf), (vp_hbm, vf), (sk_hbm, sk), (sv_hbm, sv)))
    ]
    for load in loads:
        load.start()

    barrier = pltpu.get_barrier_semaphore()

    @pl.loop(1, nz)
    def _(d):
        pl.semaphore_signal(barrier, inc=1, device_id=along_z(d), device_id_type=MESH)

    for j in range(1, plane):
        pl.semaphore_signal(barrier, inc=1, device_id=in_plane(j, 1), device_id_type=MESH)

    pack = in_a.shape[1]

    def pack_a(i, dst):
        @pl.loop(0, pack, unroll=4)
        def _(n):
            row = own_tab[i, 0, 64 + n]
            for jy in range(ny):
                dst[i, n, jy] = q[row, y_at[jy]]

    pack_a(0, in_a)

    @pl.loop(1, nz)
    def _(i):
        pack_a(i, out_a)

    pl.semaphore_wait(barrier, nz - 1 + plane - 1)

    def a_copy(i):
        return pltpu.make_async_remote_copy(
            out_a.at[i], in_a.at[i], a_send.at[i], a_recv.at[i],
            device_id=along_z(step_offset(i, nz)), device_id_type=MESH,
        )

    def t_copy(i):
        return pltpu.make_async_remote_copy(
            tab.at[i], in_tab.at[i], t_send.at[i], t_recv.at[i],
            device_id=along_z(step_offset(i, nz)), device_id_type=MESH,
        )

    def start_b(i, table):
        rows_a[...] = in_a[i]

        @pl.loop(0, nx * nc, unroll=4)
        def _(k):
            for s in range(CAP):
                n = table[i, 0, k * CAP + s]
                for jy in range(ny):
                    out_b[i, k * ny + jy, s] = rows_a[n, jy]

        pltpu.make_async_copy(out_b.at[i, 0], in_b.at[i, 0], b_recv.at[i]).start()

        for j in range(1, plane):
            pltpu.make_async_remote_copy(
                out_b.at[i, j], in_b.at[i, j], b_send.at[i], b_recv.at[i],
                device_id=in_plane(j, 1), device_id_type=MESH,
            ).start()

    def start_bp(i, first, last):
        if first == 0:
            pltpu.make_async_copy(out_bp.at[i, 0], in_bp.at[i, 0], bp_recv.at[i]).start()
            pltpu.make_async_copy(out_m.at[i, 0], in_m.at[i, 0], m_recv.at[i]).start()
        for j in range(max(first, 1), last):
            pltpu.make_async_remote_copy(
                out_m.at[i, j // 4], in_m.at[i, j], m_send.at[i], m_recv.at[i],
                device_id=in_plane(j, -1), device_id_type=MESH,
            ).start()
            pltpu.make_async_remote_copy(
                out_bp.at[i, j], in_bp.at[i, j], bp_send.at[i], bp_recv.at[i],
                device_id=in_plane(j, -1), device_id_type=MESH,
            ).start()

    def ap_copies(i):
        back = along_z((nz - step_offset(i, nz)) % nz)
        return (
            pltpu.make_async_remote_copy(
                out_mp.at[i], in_mp.at[i], mp_send.at[i], mp_recv.at[i],
                device_id=back, device_id_type=MESH,
            ),
            pltpu.make_async_remote_copy(
                out_ap.at[i], in_ap.at[i], ap_send.at[i], ap_recv.at[i],
                device_id=back, device_id_type=MESH,
            ),
        )

    def wait_all(ref, sem):
        pltpu.make_async_copy(ref, ref, sem).wait()

    @pl.loop(1, nz)
    def _(i):
        t_copy(i).start()

    @pl.loop(1, 1 + WINDOW)
    def _(i):
        a_copy(i).start()

    pltpu.make_async_copy(tab.at[0], in_tab.at[0], t_recv.at[0]).start()
    start_b(0, own_tab)

    loads[0].wait()
    for part in range(2 * keys // 1024):
        stage[part * 1024 : (part + 1) * 1024] = kf[part * 1024 : (part + 1) * 1024].astype(F32)
    for part in range(keys // KEY_BLOCK):
        for k in range(2):
            block = stage[pl.ds(part * 2 * KEY_BLOCK + k, KEY_BLOCK, stride=2), :]
            kc[part * KEY_BLOCK : (part + 1) * KEY_BLOCK, k * width : (k + 1) * width] = block.astype(BF16)
    loads[1].wait()
    for part in range(2 * keys // 1024):
        stage[part * 1024 : (part + 1) * 1024] = vf[part * 1024 : (part + 1) * 1024].astype(F32)
    for part in range(keys // KEY_BLOCK):
        for k in range(2):
            block = stage[pl.ds(part * 2 * KEY_BLOCK + k, KEY_BLOCK, stride=2), :]
            vt[k * width : (k + 1) * width, part * KEY_BLOCK : (part + 1) * KEY_BLOCK] = block.T.astype(BF16)
    loads[2].wait()
    loads[3].wait()

    wait_all(in_tab.at[0], t_recv.at[0])

    @pl.loop(1, nz)
    def _(i):
        t_copy(i).wait()

    to_scalars = pltpu.make_async_copy(in_tab, stab, f_sem.at[0])
    to_scalars.start()
    worst = in_tab[0]
    for i in range(1, nz):
        worst = jnp.maximum(worst, in_tab[i])
    out_f[...] = worst
    in_f[0] = worst

    for j in range(1, plane):
        pltpu.make_async_remote_copy(
            out_f, in_f.at[j], f_sem.at[1], f_sem.at[2],
            device_id=in_plane(j, 1), device_id_type=MESH,
        ).start()

    to_scalars.wait()

    kv = nk.shape[1]
    cols = sk.shape[1]
    heads = ny * GROUP
    head_of = lax.broadcasted_iota(jnp.int32, (heads, cols), 0) // PER_KV
    col = lax.broadcasted_iota(jnp.int32, (heads, cols), 1)
    own_head = head_of == col % kv

    def suffix_row(r):
        qr = q[r].reshape(heads, width)
        s = lax.dot_general(qr, sk[r], (((1,), (1,)), ((), ())), preferred_element_type=F32)
        s = jnp.where(own_head & (col < suf_len[r] * kv), s * scale, -1e30)
        new_k = jnp.broadcast_to(nk[r].astype(F32)[:, None, :], (kv, PER_KV, width)).reshape(heads, width)
        new_v = jnp.broadcast_to(nv[r].astype(F32)[:, None, :], (kv, PER_KV, width)).reshape(heads, width)
        own = jnp.sum(qr.astype(F32) * new_k, axis=1, keepdims=True) * scale
        top = jnp.maximum(jnp.max(s, axis=1, keepdims=True), own)
        w = jnp.exp2(s - top)
        own_w = jnp.exp2(own - top)
        total = jnp.sum(w, axis=1, keepdims=True) + own_w
        acc = jnp.dot(w.astype(BF16), sv[r], preferred_element_type=F32)
        acc = acc + own_w.astype(BF16).astype(F32) * new_v
        sacc[r] = (acc / total).reshape(ny, GROUP, width)
        smass[r] = jnp.broadcast_to(top + jnp.log2(total), (heads, width)).reshape(ny, GROUP, width)

    part_rows = rows // nz

    def suffix_part(i):
        @pl.loop(0, part_rows // 2)
        def _(n):
            suffix_row(i * part_rows + 2 * n)
            suffix_row(i * part_rows + 2 * n + 1)

    low_row = lax.broadcasted_iota(jnp.int32, (TILE, width), 0) % GROUP < PER_KV
    low_lane = lax.broadcasted_iota(jnp.int32, (width, TILE), 1) % GROUP < PER_KV
    senders = TILE // (CAP * GROUP)

    blocks = [slice(b, b + KEY_BLOCK) for b in range(0, keys, KEY_BLOCK)]

    def score(i, t):
        xq = in_b[i, t * senders : (t + 1) * senders].reshape(TILE, width).astype(F32)
        xq = jnp.concatenate(
            [jnp.where(low_row, xq, 0.0), jnp.where(low_row, 0.0, xq)], axis=1
        ).astype(BF16)
        top = None
        for block in blocks:
            s = lax.dot_general(kc[block], xq, (((1,), (1,)), ((), ())), preferred_element_type=F32)
            scores[t % 2, block] = s
            high = jnp.max(s, axis=0, keepdims=True)
            top = high if top is None else jnp.maximum(top, high)
        return top * scale

    def weigh(i, t, top):
        total = jnp.zeros_like(top)
        acc = jnp.zeros((2 * width, TILE), F32)
        for block in blocks:
            w = jnp.exp2(scores[t % 2, block] * scale - top)
            total = total + jnp.sum(w, axis=0, keepdims=True)
            acc = acc + jnp.dot(vt[:, block], w.astype(BF16), preferred_element_type=F32)
        o = jnp.where(low_lane, acc[:width], acc[width:]) / total
        out_bp[i, t * senders : (t + 1) * senders] = o.T.astype(BF16).reshape(senders, CAP, GROUP, width)
        mass = top + jnp.log2(total)
        for h in range(TILE // 128):
            out_m[i, t * (TILE // 128) + h] = mass[:, h * 128 : (h + 1) * 128]

    def attend(i):
        tiles = plane // senders
        top = score(i, 0)
        for t in range(tiles):
            later = score(i, t + 1) if t + 1 < tiles else None
            weigh(i, t, top)
            start_bp(i, t * senders, (t + 1) * senders)
            top = later

    mass_lane = lax.broadcasted_iota(jnp.int32, (1, 128), 1)

    def give_back(i):
        wait_all(in_bp.at[i], bp_recv.at[i])
        wait_all(in_m.at[i], m_recv.at[i])
        rows_bp[...] = in_bp[i]
        rows_m[...] = in_m[i]

        @pl.loop(0, pack, unroll=4)
        def _(n):
            k, slot = stab[i, 0, 16 + n], stab[i, 0, 32 + n]
            mass = rows_m[k * ny]
            for jy in range(ny):
                out_ap[i, n, jy] = rows_bp[k * ny + jy, slot]
                if jy > 0:
                    mass = jnp.where(mass_lane // (CAP * GROUP) == jy, rows_m[k * ny + jy], mass)
            out_mp[i, n] = mass


    suffix_part(0)
    suffix_part(1)
    wait_all(in_b.at[0], b_recv.at[0])
    attend(0)

    @pl.loop(1, nz + 2)
    def _(n):
        @pl.when(n < nz)
        def _():
            a_copy(n).wait_recv()
            start_b(n, stab)

        @pl.when(n + WINDOW < nz)
        def _():
            a_copy(n + WINDOW).start()

        @pl.when(n <= nz // 2 - 1)
        def _():
            suffix_part(2 * n)
            suffix_part(2 * n + 1)

        @pl.when((n >= 2) & (n <= nz))
        def _():
            wait_all(in_b.at[n - 1], b_recv.at[n - 1])
            attend(n - 1)

        @pl.when(n == 1)
        def _():
            give_back(0)
            pltpu.make_async_copy(out_mp.at[0], in_mp.at[0], mp_recv.at[0]).start()
            pltpu.make_async_copy(out_ap.at[0], in_ap.at[0], ap_recv.at[0]).start()

        @pl.when(n >= 3)
        def _():
            give_back(n - 2)
            for copy in ap_copies(n - 2):
                copy.start()

    wait_all(in_f.at[pl.ds(1, plane - 1)], f_sem.at[1])
    wait_all(in_f.at[pl.ds(1, plane - 1)], f_sem.at[2])
    spilled[0] = jnp.max(jnp.where(mass_lane == 48, jnp.max(in_f[...], axis=0), 0))
    wait_all(in_b.at[0, pl.ds(1, plane - 1)], b_send.at[0])
    wait_all(in_bp.at[0, pl.ds(1, plane - 1)], bp_send.at[0])
    wait_all(in_m.at[0, pl.ds(1, plane - 1)], m_send.at[0])
    wait_all(in_mp.at[0], mp_recv.at[0])
    wait_all(in_ap.at[0], ap_recv.at[0])

    @pl.loop(1, nz)
    def _(i):
        a_copy(i).wait_send()
        wait_all(in_b.at[i, pl.ds(1, plane - 1)], b_send.at[i])
        wait_all(in_bp.at[i, pl.ds(1, plane - 1)], bp_send.at[i])
        wait_all(in_m.at[i, pl.ds(1, plane - 1)], m_send.at[i])
        for copy in ap_copies(i):
            copy.wait()

    @pl.loop(0, rows, unroll=8)
    def _(r):
        gath[pl.ds(r, 1), :] = in_mp[row_i[r], row_n[r]]

    turned = gath[...].T
    for jy in range(ny):
        first = turned[jy * 32 : jy * 32 + GROUP]
        second = turned[jy * 32 + GROUP : jy * 32 + 2 * GROUP]
        pmt[jy] = jnp.where(arrival[...] == 0, first, second)

    lane = lax.broadcasted_iota(jnp.int32, (GROUP, rows), 1)

    def merge_row(r):
        i, n = row_i[r], row_n[r]
        for jy in range(ny):
            yy = y_at[jy]
            pm = jnp.sum(jnp.where(lane == r, pmt[jy], 0.0), axis=1, keepdims=True)
            gap = smass[r, yy] - pm
            e = jnp.exp2(-jnp.abs(gap))
            ahead = gap <= 0
            po = in_ap[i, n, jy].astype(F32)
            so = sacc[r, yy]
            merged = (jnp.where(ahead, 1.0, e) * po + jnp.where(ahead, e, 1.0) * so) / (1.0 + e)
            out[r, yy] = merged.astype(BF16)

    @pl.loop(0, rows // 2)
    def _(n):
        merge_row(2 * n)
        merge_row(2 * n + 1)


def wide_attend(received, key_cache, value_cache, scale_factor):
    lined = jnp.transpose(received, (3, 1, 0, 2, 4, 5))

    def per_head(packed_tuple):
        head_query, head_keys, head_values = packed_tuple

        def per_group(block_query_rows):
            scores = (
                jnp.einsum(
                    "ncgd,td->ncgt", block_query_rows, head_keys, preferred_element_type=jnp.float32
                )
                * scale_factor
            )
            highest = jnp.max(scores, axis=-1)
            weights_raw = jnp.exp(scores - highest[..., None])
            totals = jnp.sum(weights_raw, axis=-1)
            blended = jnp.einsum(
                "ncgt,td->ncgd",
                weights_raw.astype(jnp.bfloat16),
                head_values,
                preferred_element_type=jnp.float32,
            )
            return ((blended / totals[..., None]).astype(jnp.bfloat16), highest + jnp.log(totals))

        return lax.map(per_group, head_query)

    blended, log_mass = lax.map(
        per_head,
        (lined, jnp.transpose(key_cache, (1, 0, 2)), jnp.transpose(value_cache, (1, 0, 2))),
    )
    return (jnp.transpose(blended, (2, 1, 3, 0, 4, 5)), jnp.transpose(log_mass, (2, 1, 3, 0, 4)))


def wide_body(
    queries,
    prefix_id,
    suffix_len,
    prefix_keys,
    prefix_values,
    suffix_keys,
    suffix_values,
    new_keys,
    new_values,
):
    row_count, head_count, head_width = queries.shape
    kv_all = suffix_keys.shape[2]
    per_kv = head_count // kv_all
    owners = lax.axis_size("prefix")
    capacity = 2 * row_count // owners
    scale_factor = 1.0 / math.sqrt(head_width)
    target = prefix_id[:, 0]
    row_index = lax.broadcasted_iota(jnp.int32, (row_count, row_count), 0)
    col_index = lax.broadcasted_iota(jnp.int32, (row_count, row_count), 1)
    earlier = (target[None, :] == target[:, None]) & (col_index < row_index)
    arrival = jnp.sum(earlier.astype(jnp.int32), axis=1)
    position = target * capacity + arrival
    query_layout = queries.reshape(row_count, kv_all, per_kv, head_width)
    outbox = (
        jnp.zeros((owners * capacity, kv_all, per_kv, head_width), jnp.bfloat16)
        .at[position]
        .set(query_layout)
    )
    outbox = outbox.reshape(owners, 1, capacity, kv_all, per_kv, head_width)
    key_cache = prefix_keys[0]
    value_cache = prefix_values[0]
    received = lax.all_to_all(
        lax.all_to_all(outbox, "prefix", split_axis=0, concat_axis=0, tiled=True),
        "head",
        split_axis=3,
        concat_axis=1,
        tiled=True,
    )
    blended, log_mass = wide_attend(received, key_cache, value_cache, scale_factor)
    blended = lax.all_to_all(
        lax.all_to_all(blended, "prefix", split_axis=0, concat_axis=0, tiled=True),
        "head",
        split_axis=1,
        concat_axis=3,
        tiled=True,
    )
    log_mass = lax.all_to_all(
        lax.all_to_all(log_mass, "prefix", split_axis=0, concat_axis=0, tiled=True),
        "head",
        split_axis=1,
        concat_axis=3,
        tiled=True,
    )
    prefix_out = blended.reshape(owners * capacity, kv_all, per_kv, head_width)[position].astype(
        jnp.float32
    )
    prefix_mass = log_mass.reshape(owners * capacity, kv_all, per_kv)[position]
    private_scores = (
        jnp.einsum("wtfb,wmtb->wtfm", query_layout, suffix_keys, preferred_element_type=jnp.float32)
        * scale_factor
    )
    visible = (jnp.arange(suffix_keys.shape[1], dtype=jnp.int32)[None, :] < suffix_len[:, None])[
        :, None, None, :
    ]
    private_scores = jnp.where(visible, private_scores, -jnp.inf)
    own_score = (
        jnp.einsum("rkgd,rkd->rkg", query_layout, new_keys, preferred_element_type=jnp.float32)
        * scale_factor
    )
    suffix_top = jnp.maximum(jnp.max(private_scores, axis=-1), own_score)
    suffix_raw = jnp.where(visible, jnp.exp(private_scores - suffix_top[..., None]), 0.0)
    own_weight = jnp.exp(own_score - suffix_top)
    suffix_totals = jnp.sum(suffix_raw, axis=-1) + own_weight
    gathered = jnp.einsum(
        "rkgs,rskd->rkgd",
        suffix_raw.astype(jnp.bfloat16),
        suffix_values,
        preferred_element_type=jnp.float32,
    )
    gathered = (
        gathered
        + own_weight.astype(jnp.bfloat16).astype(jnp.float32)[..., None]
        * new_values.astype(jnp.float32)[:, :, None, :]
    )
    suffix_out = gathered / suffix_totals[..., None]
    suffix_mass = suffix_top + jnp.log(suffix_totals)
    ceiling = jnp.maximum(prefix_mass, suffix_mass)
    share_prefix = jnp.exp(prefix_mass - ceiling)
    share_suffix = jnp.exp(suffix_mass - ceiling)
    merged = (share_prefix[..., None] * prefix_out + share_suffix[..., None] * suffix_out) / (
        share_prefix + share_suffix
    )[..., None]
    return merged.reshape(row_count, head_count, head_width).astype(jnp.bfloat16)


def body(
    queries,
    prefix_id,
    suffix_len,
    prefix_keys,
    prefix_values,
    suffix_keys,
    suffix_values,
    new_keys,
    new_values,
):
    rows, heads, width = queries.shape
    prefixes, ny = lax.axis_size("prefix"), lax.axis_size("head")
    nx, nz, nc = axes_of(prefixes)
    plane = nx * nc * ny
    keys = prefix_keys.shape[1]
    slots, kv = suffix_keys.shape[1:3]

    me_p = lax.axis_index("prefix")
    x, z, c = me_p // (nz * nc), (me_p // nc) % nz, me_p % nc
    target = prefix_id[:, 0]
    dz = (target // nc - z) % nz
    step = jnp.where(dz == 0, 0, jnp.where(2 * dz <= nz, 2 * dz - 1, 2 * (nz - dz)))
    spot = ((target // (nz * nc) - x) % nx) * nc + (target - c) % nc
    r_index = lax.broadcasted_iota(jnp.int32, (rows, rows), 0)
    c_index = lax.broadcasted_iota(jnp.int32, (rows, rows), 1)
    earlier = c_index < r_index
    arrival = jnp.sum(((target[None, :] == target[:, None]) & earlier).astype(jnp.int32), axis=1)
    rank = jnp.sum(((step[None, :] == step[:, None]) & earlier).astype(jnp.int32), axis=1)
    row_n = jnp.minimum(rank, PACK - 1)
    spill = (rank >= PACK).astype(jnp.int32)
    shape = (nz, 128, rows)
    t_step = lax.broadcasted_iota(jnp.int32, shape, 0)
    t_lane = lax.broadcasted_iota(jnp.int32, shape, 1)
    field, entry = t_lane // 16, t_lane % 16
    mine = (step[None, None, :] == t_step) & (spill == 0)[None, None, :]
    by_slot = mine & ((spot * CAP + arrival)[None, None, :] == entry)
    by_rank = mine & (rank[None, None, :] == entry)
    r_value = lax.broadcasted_iota(jnp.int32, shape, 2)
    value = jnp.where((field == 0) & by_slot, rank[None, None, :], 0)
    value = jnp.where((field == 1) & by_rank, spot[None, None, :], value)
    value = jnp.where((field == 2) & by_rank, arrival[None, None, :], value)
    value = jnp.where((field == 3) & (entry == 0), spill[None, None, :], value)
    value = jnp.where((field == 4) & by_rank, r_value, value)
    table = jnp.sum(value, axis=2)[:, None, :]

    smem = pl.BlockSpec(memory_space=pltpu.SMEM)
    vmem = pl.BlockSpec(memory_space=pltpu.VMEM)
    hbm = pl.BlockSpec(memory_space=pl.ANY)
    message = (CAP, GROUP, width)
    dma = pltpu.SemaphoreType.DMA
    attended, spilled = pl.pallas_call(
        functools.partial(kernel, (nx, nz, nc, ny)),
        out_shape=(
            jax.ShapeDtypeStruct((rows, ny, GROUP, width), BF16),
            jax.ShapeDtypeStruct((1,), jnp.int32),
        ),
        in_specs=[smem] * 4 + [vmem] * 3 + [hbm] * 4 + [vmem] * 2,
        out_specs=(vmem, smem),
        scratch_shapes=[
            pltpu.VMEM((nz, PACK, ny, GROUP, width), BF16),
            pltpu.VMEM((nz, PACK, ny, GROUP, width), BF16),
            pltpu.VMEM((nz, plane) + message, BF16),
            pltpu.VMEM((nz, plane) + message, BF16),
            pltpu.VMEM((nz, plane) + message, BF16),
            pltpu.VMEM((nz, plane) + message, BF16),
            pltpu.VMEM((nz, PACK, ny, GROUP, width), BF16),
            pltpu.VMEM((nz, PACK, ny, GROUP, width), BF16),
            pltpu.VMEM((nz, plane // 4, 1, 128), F32),
            pltpu.VMEM((nz, plane, 1, 128), F32),
            pltpu.VMEM((nz, PACK, 1, 128), F32),
            pltpu.VMEM((nz, PACK, 1, 128), F32),
            pltpu.VMEM((nz, 1, 128), jnp.int32),
            pltpu.SMEM((nz, 1, 128), jnp.int32),
            pltpu.VMEM((1, 128), jnp.int32),
            pltpu.VMEM((plane, 1, 128), jnp.int32),
            pltpu.VMEM((PACK, ny, GROUP, width), BF16),
            pltpu.VMEM((plane,) + message, BF16),
            pltpu.VMEM((plane, 1, 128), F32),
            pltpu.VMEM((rows, slots * kv, width), BF16),
            pltpu.VMEM((rows, slots * kv, width), BF16),
            pltpu.VMEM((2 * keys, width), BF16),
            pltpu.VMEM((2 * keys, width), BF16),
            pltpu.VMEM((2 * keys, width), F32),
            pltpu.VMEM((keys, 2 * width), BF16),
            pltpu.VMEM((2 * width, keys), BF16),
            pltpu.VMEM((2, keys, TILE), F32),
            pltpu.VMEM((rows, ny, GROUP, width), F32),
            pltpu.VMEM((rows, ny, GROUP, width), F32),
            pltpu.VMEM((rows, 128), F32),
            pltpu.VMEM((ny, GROUP, rows), F32),
            dma((4,)),
        ]
        + [dma((nz,))] * 14
        + [dma((3,))],
        compiler_params=pltpu.CompilerParams(
            collective_id=0, has_side_effects=True, vmem_limit_bytes=56 * 2**20
        ),
    )(
        table,
        step,
        row_n,
        suffix_len,
        arrival[None, :],
        table,
        queries.reshape(rows, ny, GROUP, width),
        prefix_keys.reshape(2 * keys, width),
        prefix_values.reshape(2 * keys, width),
        suffix_keys.reshape(rows, slots * kv, width),
        suffix_values.reshape(rows, slots * kv, width),
        new_keys,
        new_values,
    )
    args = (
        queries,
        prefix_id,
        suffix_len,
        prefix_keys,
        prefix_values,
        suffix_keys,
        suffix_values,
        new_keys,
        new_values,
    )
    return lax.cond(
        spilled[0] > 0,
        wide_body,
        lambda *_: attended.reshape(rows, heads, width),
        *args,
    )


def solution(mesh):
    rows = P(("prefix", "head"))
    cache = P("prefix", None, "head", None)
    return jax.shard_map(
        body,
        mesh=mesh,
        in_specs=(rows, rows, rows, cache, cache, rows, rows, rows, rows),
        out_specs=rows,
        check_vma=False,
    )
```

```python
import functools
import math

import jax
import jax.numpy as jnp
from jax import lax
from jax.experimental import pallas as pl
from jax.experimental.pallas import tpu as pltpu
from jax.sharding import PartitionSpec as P

MESH = pl.DeviceIdType.MESH
BF16 = jnp.bfloat16
F32 = jnp.float32
LOG2E = 1.4426950408889634
CAP = 2
PER_KV = 8
GROUP = 16
KEY_BLOCK = 256
TILE = 256
WINDOW = 7
PACK = 12


def axes_of(prefixes):
    return {64: (4, 8, 2)}[prefixes]


def step_offset(i, nz):
    odd = i % 2
    return odd * ((i + 1) // 2) + (1 - odd) * ((nz - i // 2) % nz)


def kernel(
    sizes,
    own_tab,
    row_i,
    row_n,
    suf_len,
    arrival,
    tab,
    q,
    kp_hbm,
    vp_hbm,
    sk_hbm,
    sv_hbm,
    nk,
    nv,
    out,
    spilled,
    out_a,
    in_a,
    out_b,
    in_b,
    out_bp,
    in_bp,
    out_ap,
    in_ap,
    out_m,
    in_m,
    out_mp,
    in_mp,
    in_tab,
    stab,
    out_f,
    in_f,
    rows_a,
    rows_bp,
    rows_m,
    sk,
    sv,
    kf,
    vf,
    stage,
    kc,
    vt,
    scores,
    sacc,
    smass,
    gath,
    pmt,
    load_sem,
    a_send,
    a_recv,
    b_send,
    b_recv,
    bp_send,
    bp_recv,
    m_send,
    m_recv,
    ap_send,
    ap_recv,
    mp_send,
    mp_recv,
    t_send,
    t_recv,
    f_sem,
):
    nx, nz, nc, ny = sizes
    plane = nx * nc * ny
    rows = q.shape[0]
    width = q.shape[-1]
    keys = kc.shape[0]
    scale = LOG2E / math.sqrt(width)
    me_p, y = lax.axis_index("prefix"), lax.axis_index("head")
    x, z, c = me_p // (nz * nc), (me_p // nc) % nz, me_p % nc

    def at(x_, z_, c_, y_):
        return ((x_ * nz + z_) * nc + c_, y_)

    def along_z(d):
        return at(x, (z + d) % nz, c, y)

    offsets = [(jx, jc, jy) for jx in range(nx) for jc in range(nc) for jy in range(ny)]
    y_at = [(y + jy) % ny for jy in range(ny)]
    column = {
        (sign, jx, jc): (((x + nx + sign * jx) % nx) * nz + z) * nc + (c + jc) % nc
        for sign in (1, -1)
        for jx in range(nx)
        for jc in range(nc)
    }

    def in_plane(j, sign):
        jx, jc, jy = offsets[j]
        return column[sign, jx, jc], y_at[sign * jy % ny]

    loads = [
        pltpu.make_async_copy(s, d, load_sem.at[n])
        for n, (s, d) in enumerate(((kp_hbm, kf), (vp_hbm, vf), (sk_hbm, sk), (sv_hbm, sv)))
    ]
    for load in loads:
        load.start()

    barrier = pltpu.get_barrier_semaphore()

    @pl.loop(1, nz)
    def _(d):
        pl.semaphore_signal(barrier, inc=1, device_id=along_z(d), device_id_type=MESH)

    for j in range(1, plane):
        pl.semaphore_signal(barrier, inc=1, device_id=in_plane(j, 1), device_id_type=MESH)

    pack = in_a.shape[1]

    def pack_a(i, dst):
        @pl.loop(0, pack, unroll=4)
        def _(n):
            row = own_tab[i, 0, 64 + n]
            for jy in range(ny):
                dst[i, n, jy] = q[row, y_at[jy]]

    pack_a(0, in_a)

    @pl.loop(1, nz)
    def _(i):
        pack_a(i, out_a)

    pl.semaphore_wait(barrier, nz - 1 + plane - 1)

    def a_copy(i):
        return pltpu.make_async_remote_copy(
            out_a.at[i], in_a.at[i], a_send.at[i], a_recv.at[i],
            device_id=along_z(step_offset(i, nz)), device_id_type=MESH,
        )

    def t_copy(i):
        return pltpu.make_async_remote_copy(
            tab.at[i], in_tab.at[i], t_send.at[i], t_recv.at[i],
            device_id=along_z(step_offset(i, nz)), device_id_type=MESH,
        )

    def start_b(i, table):
        rows_a[...] = in_a[i]

        @pl.loop(0, nx * nc, unroll=4)
        def _(k):
            for s in range(CAP):
                n = table[i, 0, k * CAP + s]
                for jy in range(ny):
                    out_b[i, k * ny + jy, s] = rows_a[n, jy]

        pltpu.make_async_copy(out_b.at[i, 0], in_b.at[i, 0], b_recv.at[i]).start()

        for j in range(1, plane):
            pltpu.make_async_remote_copy(
                out_b.at[i, j], in_b.at[i, j], b_send.at[i], b_recv.at[i],
                device_id=in_plane(j, 1), device_id_type=MESH,
            ).start()

    def start_m(g):
        pltpu.make_async_copy(out_m.at[g, 0], in_m.at[g, 0], m_recv.at[g]).start()
        for j in range(1, plane):
            pltpu.make_async_remote_copy(
                out_m.at[g, j // 4], in_m.at[g, j], m_send.at[g], m_recv.at[g],
                device_id=in_plane(j, -1), device_id_type=MESH,
            ).start()

    def start_bp(i, first, last):
        if first == 0:
            pltpu.make_async_copy(out_bp.at[i, 0], in_bp.at[i, 0], bp_recv.at[i]).start()
        for j in range(max(first, 1), last):
            pltpu.make_async_remote_copy(
                out_bp.at[i, j], in_bp.at[i, j], bp_send.at[i], bp_recv.at[i],
                device_id=in_plane(j, -1), device_id_type=MESH,
            ).start()

    def ap_copy(i):
        return pltpu.make_async_remote_copy(
            out_ap.at[i], in_ap.at[i], ap_send.at[i], ap_recv.at[i],
            device_id=along_z((nz - step_offset(i, nz)) % nz), device_id_type=MESH,
        )

    def mp_copy(i):
        return pltpu.make_async_remote_copy(
            out_mp.at[i], in_mp.at[i], mp_send.at[i], mp_recv.at[i],
            device_id=along_z((nz - step_offset(i, nz)) % nz), device_id_type=MESH,
        )

    def wait_all(ref, sem):
        pltpu.make_async_copy(ref, ref, sem).wait()

    @pl.loop(1, nz)
    def _(i):
        t_copy(i).start()

    @pl.loop(1, 1 + WINDOW)
    def _(i):
        a_copy(i).start()

    pltpu.make_async_copy(tab.at[0], in_tab.at[0], t_recv.at[0]).start()
    start_b(0, own_tab)

    loads[0].wait()
    for part in range(2 * keys // 1024):
        stage[part * 1024 : (part + 1) * 1024] = kf[part * 1024 : (part + 1) * 1024].astype(F32)
    for part in range(keys // KEY_BLOCK):
        for k in range(2):
            block = stage[pl.ds(part * 2 * KEY_BLOCK + k, KEY_BLOCK, stride=2), :]
            kc[part * KEY_BLOCK : (part + 1) * KEY_BLOCK, k * width : (k + 1) * width] = block.astype(BF16)
    loads[1].wait()
    for part in range(2 * keys // 1024):
        stage[part * 1024 : (part + 1) * 1024] = vf[part * 1024 : (part + 1) * 1024].astype(F32)
    for part in range(keys // KEY_BLOCK):
        for k in range(2):
            block = stage[pl.ds(part * 2 * KEY_BLOCK + k, KEY_BLOCK, stride=2), :]
            vt[k * width : (k + 1) * width, part * KEY_BLOCK : (part + 1) * KEY_BLOCK] = block.T.astype(BF16)
    loads[2].wait()
    loads[3].wait()

    wait_all(in_tab.at[0], t_recv.at[0])

    @pl.loop(1, nz)
    def _(i):
        t_copy(i).wait()

    to_scalars = pltpu.make_async_copy(in_tab, stab, f_sem.at[0])
    to_scalars.start()
    worst = in_tab[0]
    for i in range(1, nz):
        worst = jnp.maximum(worst, in_tab[i])
    out_f[...] = worst
    in_f[0] = worst

    for j in range(1, plane):
        pltpu.make_async_remote_copy(
            out_f, in_f.at[j], f_sem.at[1], f_sem.at[2],
            device_id=in_plane(j, 1), device_id_type=MESH,
        ).start()

    to_scalars.wait()

    kv = nk.shape[1]
    cols = sk.shape[1]
    heads = ny * GROUP
    head_of = lax.broadcasted_iota(jnp.int32, (heads, cols), 0) // PER_KV
    col = lax.broadcasted_iota(jnp.int32, (heads, cols), 1)
    own_head = head_of == col % kv

    def suffix_row(r):
        qr = q[r].reshape(heads, width)
        s = lax.dot_general(qr, sk[r], (((1,), (1,)), ((), ())), preferred_element_type=F32)
        s = jnp.where(own_head & (col < suf_len[r] * kv), s * scale, -1e30)
        new_k = jnp.broadcast_to(nk[r].astype(F32)[:, None, :], (kv, PER_KV, width)).reshape(heads, width)
        new_v = jnp.broadcast_to(nv[r].astype(F32)[:, None, :], (kv, PER_KV, width)).reshape(heads, width)
        own = jnp.sum(qr.astype(F32) * new_k, axis=1, keepdims=True) * scale
        top = jnp.maximum(jnp.max(s, axis=1, keepdims=True), own)
        w = jnp.exp2(s - top)
        own_w = jnp.exp2(own - top)
        total = jnp.sum(w, axis=1, keepdims=True) + own_w
        acc = jnp.dot(w.astype(BF16), sv[r], preferred_element_type=F32)
        acc = acc + own_w.astype(BF16).astype(F32) * new_v
        sacc[r] = (acc / total).reshape(ny, GROUP, width)
        smass[r] = jnp.broadcast_to(top + jnp.log2(total), (heads, width)).reshape(ny, GROUP, width)

    part_rows = rows // nz

    def suffix_part(i):
        @pl.loop(0, part_rows // 2)
        def _(n):
            suffix_row(i * part_rows + 2 * n)
            suffix_row(i * part_rows + 2 * n + 1)

    low_row = lax.broadcasted_iota(jnp.int32, (TILE, width), 0) % GROUP < PER_KV
    low_lane = lax.broadcasted_iota(jnp.int32, (width, TILE), 1) % GROUP < PER_KV
    senders = TILE // (CAP * GROUP)

    blocks = [slice(b, b + KEY_BLOCK) for b in range(0, keys, KEY_BLOCK)]

    def score(i, t):
        xq = in_b[i, t * senders : (t + 1) * senders].reshape(TILE, width).astype(F32)
        xq = jnp.concatenate(
            [jnp.where(low_row, xq, 0.0), jnp.where(low_row, 0.0, xq)], axis=1
        ).astype(BF16)
        top = None
        for block in blocks:
            s = lax.dot_general(kc[block], xq, (((1,), (1,)), ((), ())), preferred_element_type=F32)
            scores[t % 2, block] = s
            high = jnp.max(s, axis=0, keepdims=True)
            top = high if top is None else jnp.maximum(top, high)
        return top * scale

    def weigh(i, t, top):
        total = jnp.zeros_like(top)
        acc = jnp.zeros((2 * width, TILE), F32)
        for block in blocks:
            w = jnp.exp2(scores[t % 2, block] * scale - top)
            total = total + jnp.sum(w, axis=0, keepdims=True)
            acc = acc + jnp.dot(vt[:, block], w.astype(BF16), preferred_element_type=F32)
        o = jnp.where(low_lane, acc[:width], acc[width:]) / total
        out_bp[i, t * senders : (t + 1) * senders] = o.T.astype(BF16).reshape(senders, CAP, GROUP, width)
        mass = top + jnp.log2(total)
        for h in range(TILE // 128):
            out_m[i // 2, t * (TILE // 128) + h, i % 2] = mass[:, h * 128 : (h + 1) * 128]

    def attend(i):
        tiles = plane // senders
        top = score(i, 0)
        for t in range(tiles):
            later = score(i, t + 1) if t + 1 < tiles else None
            weigh(i, t, top)
            start_bp(i, t * senders, (t + 1) * senders)
            top = later

    mass_lane = lax.broadcasted_iota(jnp.int32, (1, 128), 1)

    def give_masses(g):
        wait_all(in_m.at[g], m_recv.at[g])
        rows_m[...] = in_m[g]
        for h in range(2):
            i = 2 * g + h

            @pl.loop(0, pack, unroll=4)
            def _(n):
                k = stab[i, 0, 16 + n]
                mass = rows_m[k * ny, h]
                for jy in range(1, ny):
                    mass = jnp.where(mass_lane // (CAP * GROUP) == jy, rows_m[k * ny + jy, h], mass)
                out_mp[i, n] = mass

    def give_back(i):
        wait_all(in_bp.at[i], bp_recv.at[i])
        rows_bp[...] = in_bp[i]

        @pl.loop(0, pack, unroll=4)
        def _(n):
            k, slot = stab[i, 0, 16 + n], stab[i, 0, 32 + n]
            for jy in range(ny):
                out_ap[i, n, jy] = rows_bp[k * ny + jy, slot]


    suffix_part(0)
    suffix_part(1)
    wait_all(in_b.at[0], b_recv.at[0])
    attend(0)

    @pl.loop(1, nz + 2)
    def _(n):
        @pl.when(n < nz)
        def _():
            a_copy(n).wait_recv()
            start_b(n, stab)

        @pl.when(n + WINDOW < nz)
        def _():
            a_copy(n + WINDOW).start()

        @pl.when(n <= nz // 2 - 1)
        def _():
            suffix_part(2 * n)
            suffix_part(2 * n + 1)

        @pl.when((n >= 2) & (n <= nz))
        def _():
            wait_all(in_b.at[n - 1], b_recv.at[n - 1])
            attend(n - 1)

            @pl.when(n % 2 == 0)
            def _():
                start_m((n - 1) // 2)

        @pl.when(n == 1)
        def _():
            give_back(0)
            pltpu.make_async_copy(out_ap.at[0], in_ap.at[0], ap_recv.at[0]).start()

        @pl.when(n >= 3)
        def _():
            give_back(n - 2)
            ap_copy(n - 2).start()

        @pl.when((n >= 3) & (n % 2 == 1))
        def _():
            g = (n - 3) // 2
            give_masses(g)
            mp_copy(2 * g + 1).start()

            @pl.when(g > 0)
            def _():
                mp_copy(2 * g).start()

            @pl.when(g == 0)
            def _():
                pltpu.make_async_copy(out_mp.at[0], in_mp.at[0], mp_recv.at[0]).start()

    wait_all(in_f.at[pl.ds(1, plane - 1)], f_sem.at[1])
    wait_all(in_f.at[pl.ds(1, plane - 1)], f_sem.at[2])
    spilled[0] = jnp.max(jnp.where(mass_lane == 48, jnp.max(in_f[...], axis=0), 0))
    wait_all(in_b.at[0, pl.ds(1, plane - 1)], b_send.at[0])
    wait_all(in_bp.at[0, pl.ds(1, plane - 1)], bp_send.at[0])
    wait_all(in_mp.at[0], mp_recv.at[0])
    wait_all(in_ap.at[0], ap_recv.at[0])

    @pl.loop(1, nz)
    def _(i):
        a_copy(i).wait_send()
        wait_all(in_b.at[i, pl.ds(1, plane - 1)], b_send.at[i])
        wait_all(in_bp.at[i, pl.ds(1, plane - 1)], bp_send.at[i])
        ap_copy(i).wait()
        mp_copy(i).wait()

    @pl.loop(0, nz // 2)
    def _(g):
        wait_all(in_m.at[g, pl.ds(1, plane - 1)], m_send.at[g])

    @pl.loop(0, rows, unroll=8)
    def _(r):
        gath[pl.ds(r, 1), :] = in_mp[row_i[r], jnp.minimum(row_n[r], pack - 1)]

    turned = gath[...].T
    for jy in range(ny):
        first = turned[jy * 32 : jy * 32 + GROUP]
        second = turned[jy * 32 + GROUP : jy * 32 + 2 * GROUP]
        pmt[jy] = jnp.where(arrival[...] == 0, first, second)

    lane = lax.broadcasted_iota(jnp.int32, (GROUP, rows), 1)

    def merge_row(r):
        i, n = row_i[r], jnp.minimum(row_n[r], pack - 1)
        for jy in range(ny):
            yy = y_at[jy]
            pm = jnp.sum(jnp.where(lane == r, pmt[jy], 0.0), axis=1, keepdims=True)
            gap = smass[r, yy] - pm
            e = jnp.exp2(-jnp.abs(gap))
            ahead = gap <= 0
            po = in_ap[i, n, jy].astype(F32)
            so = sacc[r, yy]
            merged = (jnp.where(ahead, 1.0, e) * po + jnp.where(ahead, e, 1.0) * so) / (1.0 + e)
            out[r, yy] = merged.astype(BF16)

    @pl.loop(0, rows // 2)
    def _(n):
        merge_row(2 * n)
        merge_row(2 * n + 1)


def wide_attend(received, key_cache, value_cache, scale_factor):
    lined = jnp.transpose(received, (3, 1, 0, 2, 4, 5))

    def per_head(packed_tuple):
        head_query, head_keys, head_values = packed_tuple

        def per_group(block_query_rows):
            scores = (
                jnp.einsum(
                    "ncgd,td->ncgt", block_query_rows, head_keys, preferred_element_type=jnp.float32
                )
                * scale_factor
            )
            highest = jnp.max(scores, axis=-1)
            weights_raw = jnp.exp(scores - highest[..., None])
            totals = jnp.sum(weights_raw, axis=-1)
            blended = jnp.einsum(
                "ncgt,td->ncgd",
                weights_raw.astype(jnp.bfloat16),
                head_values,
                preferred_element_type=jnp.float32,
            )
            return ((blended / totals[..., None]).astype(jnp.bfloat16), highest + jnp.log(totals))

        return lax.map(per_group, head_query)

    blended, log_mass = lax.map(
        per_head,
        (lined, jnp.transpose(key_cache, (1, 0, 2)), jnp.transpose(value_cache, (1, 0, 2))),
    )
    return (jnp.transpose(blended, (2, 1, 3, 0, 4, 5)), jnp.transpose(log_mass, (2, 1, 3, 0, 4)))


def wide_body(
    queries,
    prefix_id,
    suffix_len,
    prefix_keys,
    prefix_values,
    suffix_keys,
    suffix_values,
    new_keys,
    new_values,
):
    row_count, head_count, head_width = queries.shape
    kv_all = suffix_keys.shape[2]
    per_kv = head_count // kv_all
    owners = lax.axis_size("prefix")
    capacity = 2 * row_count // owners
    scale_factor = 1.0 / math.sqrt(head_width)
    target = prefix_id[:, 0]
    row_index = lax.broadcasted_iota(jnp.int32, (row_count, row_count), 0)
    col_index = lax.broadcasted_iota(jnp.int32, (row_count, row_count), 1)
    earlier = (target[None, :] == target[:, None]) & (col_index < row_index)
    arrival = jnp.sum(earlier.astype(jnp.int32), axis=1)
    position = target * capacity + arrival
    query_layout = queries.reshape(row_count, kv_all, per_kv, head_width)
    outbox = (
        jnp.zeros((owners * capacity, kv_all, per_kv, head_width), jnp.bfloat16)
        .at[position]
        .set(query_layout)
    )
    outbox = outbox.reshape(owners, 1, capacity, kv_all, per_kv, head_width)
    key_cache = prefix_keys[0]
    value_cache = prefix_values[0]
    received = lax.all_to_all(
        lax.all_to_all(outbox, "prefix", split_axis=0, concat_axis=0, tiled=True),
        "head",
        split_axis=3,
        concat_axis=1,
        tiled=True,
    )
    blended, log_mass = wide_attend(received, key_cache, value_cache, scale_factor)
    blended = lax.all_to_all(
        lax.all_to_all(blended, "prefix", split_axis=0, concat_axis=0, tiled=True),
        "head",
        split_axis=1,
        concat_axis=3,
        tiled=True,
    )
    log_mass = lax.all_to_all(
        lax.all_to_all(log_mass, "prefix", split_axis=0, concat_axis=0, tiled=True),
        "head",
        split_axis=1,
        concat_axis=3,
        tiled=True,
    )
    prefix_out = blended.reshape(owners * capacity, kv_all, per_kv, head_width)[position].astype(
        jnp.float32
    )
    prefix_mass = log_mass.reshape(owners * capacity, kv_all, per_kv)[position]
    private_scores = (
        jnp.einsum("wtfb,wmtb->wtfm", query_layout, suffix_keys, preferred_element_type=jnp.float32)
        * scale_factor
    )
    visible = (jnp.arange(suffix_keys.shape[1], dtype=jnp.int32)[None, :] < suffix_len[:, None])[
        :, None, None, :
    ]
    private_scores = jnp.where(visible, private_scores, -jnp.inf)
    own_score = (
        jnp.einsum("rkgd,rkd->rkg", query_layout, new_keys, preferred_element_type=jnp.float32)
        * scale_factor
    )
    suffix_top = jnp.maximum(jnp.max(private_scores, axis=-1), own_score)
    suffix_raw = jnp.where(visible, jnp.exp(private_scores - suffix_top[..., None]), 0.0)
    own_weight = jnp.exp(own_score - suffix_top)
    suffix_totals = jnp.sum(suffix_raw, axis=-1) + own_weight
    gathered = jnp.einsum(
        "rkgs,rskd->rkgd",
        suffix_raw.astype(jnp.bfloat16),
        suffix_values,
        preferred_element_type=jnp.float32,
    )
    gathered = (
        gathered
        + own_weight.astype(jnp.bfloat16).astype(jnp.float32)[..., None]
        * new_values.astype(jnp.float32)[:, :, None, :]
    )
    suffix_out = gathered / suffix_totals[..., None]
    suffix_mass = suffix_top + jnp.log(suffix_totals)
    ceiling = jnp.maximum(prefix_mass, suffix_mass)
    share_prefix = jnp.exp(prefix_mass - ceiling)
    share_suffix = jnp.exp(suffix_mass - ceiling)
    merged = (share_prefix[..., None] * prefix_out + share_suffix[..., None] * suffix_out) / (
        share_prefix + share_suffix
    )[..., None]
    return merged.reshape(row_count, head_count, head_width).astype(jnp.bfloat16)


def body(
    queries,
    prefix_id,
    suffix_len,
    prefix_keys,
    prefix_values,
    suffix_keys,
    suffix_values,
    new_keys,
    new_values,
):
    rows, heads, width = queries.shape
    prefixes, ny = lax.axis_size("prefix"), lax.axis_size("head")
    nx, nz, nc = axes_of(prefixes)
    plane = nx * nc * ny
    keys = prefix_keys.shape[1]
    slots, kv = suffix_keys.shape[1:3]

    me_p = lax.axis_index("prefix")
    x, z, c = me_p // (nz * nc), (me_p // nc) % nz, me_p % nc
    target = prefix_id[:, 0]
    dz = (target // nc - z) % nz
    step = jnp.where(dz == 0, 0, jnp.where(2 * dz <= nz, 2 * dz - 1, 2 * (nz - dz)))
    spot = ((target // (nz * nc) - x) % nx) * nc + (target - c) % nc
    r_index = lax.broadcasted_iota(jnp.int32, (rows, rows), 0)
    c_index = lax.broadcasted_iota(jnp.int32, (rows, rows), 1)
    earlier = c_index < r_index
    arrival = jnp.sum(((target[None, :] == target[:, None]) & earlier).astype(jnp.int32), axis=1)
    rank = jnp.sum(((step[None, :] == step[:, None]) & earlier).astype(jnp.int32), axis=1)
    spill = (rank >= PACK).astype(jnp.int32)
    shape = (nz, 128, rows)
    t_step = lax.broadcasted_iota(jnp.int32, shape, 0)
    t_lane = lax.broadcasted_iota(jnp.int32, shape, 1)
    field, entry = t_lane // 16, t_lane % 16
    mine = (step[None, None, :] == t_step) & (spill == 0)[None, None, :]
    by_slot = mine & ((spot * CAP + arrival)[None, None, :] == entry)
    by_rank = mine & (rank[None, None, :] == entry)
    r_value = lax.broadcasted_iota(jnp.int32, shape, 2)
    value = jnp.where((field == 0) & by_slot, rank[None, None, :], 0)
    value = jnp.where((field == 1) & by_rank, spot[None, None, :], value)
    value = jnp.where((field == 2) & by_rank, arrival[None, None, :], value)
    value = jnp.where((field == 3) & (entry == 0), spill[None, None, :], value)
    value = jnp.where((field == 4) & by_rank, r_value, value)
    table = jnp.sum(value, axis=2)[:, None, :]

    smem = pl.BlockSpec(memory_space=pltpu.SMEM)
    vmem = pl.BlockSpec(memory_space=pltpu.VMEM)
    hbm = pl.BlockSpec(memory_space=pl.ANY)
    message = (CAP, GROUP, width)
    dma = pltpu.SemaphoreType.DMA
    attended, spilled = pl.pallas_call(
        functools.partial(kernel, (nx, nz, nc, ny)),
        out_shape=(
            jax.ShapeDtypeStruct((rows, ny, GROUP, width), BF16),
            jax.ShapeDtypeStruct((1,), jnp.int32),
        ),
        in_specs=[smem] * 4 + [vmem] * 3 + [hbm] * 4 + [vmem] * 2,
        out_specs=(vmem, smem),
        scratch_shapes=[
            pltpu.VMEM((nz, PACK, ny, GROUP, width), BF16),
            pltpu.VMEM((nz, PACK, ny, GROUP, width), BF16),
            pltpu.VMEM((nz, plane) + message, BF16),
            pltpu.VMEM((nz, plane) + message, BF16),
            pltpu.VMEM((nz, plane) + message, BF16),
            pltpu.VMEM((nz, plane) + message, BF16),
            pltpu.VMEM((nz, PACK, ny, GROUP, width), BF16),
            pltpu.VMEM((nz, PACK, ny, GROUP, width), BF16),
            pltpu.VMEM((nz // 2, plane // 4, 2, 1, 128), F32),
            pltpu.VMEM((nz // 2, plane, 2, 1, 128), F32),
            pltpu.VMEM((nz, PACK, 1, 128), F32),
            pltpu.VMEM((nz, PACK, 1, 128), F32),
            pltpu.VMEM((nz, 1, 128), jnp.int32),
            pltpu.SMEM((nz, 1, 128), jnp.int32),
            pltpu.VMEM((1, 128), jnp.int32),
            pltpu.VMEM((plane, 1, 128), jnp.int32),
            pltpu.VMEM((PACK, ny, GROUP, width), BF16),
            pltpu.VMEM((plane,) + message, BF16),
            pltpu.VMEM((plane, 2, 1, 128), F32),
            pltpu.VMEM((rows, slots * kv, width), BF16),
            pltpu.VMEM((rows, slots * kv, width), BF16),
            pltpu.VMEM((2 * keys, width), BF16),
            pltpu.VMEM((2 * keys, width), BF16),
            pltpu.VMEM((2 * keys, width), F32),
            pltpu.VMEM((keys, 2 * width), BF16),
            pltpu.VMEM((2 * width, keys), BF16),
            pltpu.VMEM((2, keys, TILE), F32),
            pltpu.VMEM((rows, ny, GROUP, width), F32),
            pltpu.VMEM((rows, ny, GROUP, width), F32),
            pltpu.VMEM((rows, 128), F32),
            pltpu.VMEM((ny, GROUP, rows), F32),
            dma((4,)),
        ]
        + [dma((nz,))] * 14
        + [dma((3,))],
        compiler_params=pltpu.CompilerParams(
            collective_id=0, has_side_effects=True, vmem_limit_bytes=56 * 2**20
        ),
    )(
        table,
        step,
        rank,
        suffix_len,
        arrival[None, :],
        table,
        queries.reshape(rows, ny, GROUP, width),
        prefix_keys.reshape(2 * keys, width),
        prefix_values.reshape(2 * keys, width),
        suffix_keys.reshape(rows, slots * kv, width),
        suffix_values.reshape(rows, slots * kv, width),
        new_keys,
        new_values,
    )
    args = (
        queries,
        prefix_id,
        suffix_len,
        prefix_keys,
        prefix_values,
        suffix_keys,
        suffix_values,
        new_keys,
        new_values,
    )
    return lax.cond(
        spilled[0] > 0,
        wide_body,
        lambda *_: attended.reshape(rows, heads, width),
        *args,
    )


def solution(mesh):
    rows = P(("prefix", "head"))
    cache = P("prefix", None, "head", None)
    return jax.shard_map(
        body,
        mesh=mesh,
        in_specs=(rows, rows, rows, cache, cache, rows, rows, rows, rows),
        out_specs=rows,
        check_vma=False,
    )
```
